512 devices in a mesh: rep: 32 (over x, y), shard: 16 (over z, core).
Axes of the slice: x: 4, y: 8, z: 8, core: 2. Of those that a mesh axis runs over, the one named last changes fastest.
Arguments:
- token_pool: bfloat16 [32, 384, 2048], P('rep'), may hold values from -6 to 6
- row_index: int32 [32, 8, 1, 512], P('rep'), may hold values from 0 to 383
- weights: bfloat16 [1, 2048, 4096], P(None, None, 'shard'), may hold values from -4 to 4
- targets: bfloat16 [32, 1, 512, 4096], P('rep', None, None, 'shard'), may hold values from -2 to 2
Outputs:
- new_weights: bfloat16 [1, 2048, 4096], P(None, None, 'shard')
The draws below stay inside these ranges and needn't reach their ends.
All inputs are finite; a program needn't handle non-finite values.
Results may differ from the reference program's by a relative error of at most 0.013.
Values may be sent and summed in bfloat16 or wider, within the bound.
A program may use at most 64 MiB of HBM per device.

```python
import math
import jax
import jax.numpy as jnp
from jax import lax

D = 2048
FF = 512
ROWS = 128
POOL = 384
STEPS = 4
EXP_LOCAL = 1
REPLICAS = 32
LEVELS = 5
BLOCKS = 8


def draw_token_pool(key, part):
    key = jax.random.fold_in(key, 11)
    sign_key, amp_key, column_key, size_key, noise_key = jax.random.split(key, 5)
    place = jnp.arange(D, dtype=jnp.float32) / (D - 1.0)
    odd_column = (jnp.arange(D, dtype=jnp.int32) % 2 == 1).astype(jnp.float32)
    order = jax.random.permutation(sign_key, REPLICAS)
    replica_sign = jnp.where(order < REPLICAS // 2, 1.0, -1.0).astype(jnp.float32)
    replica_amp = jnp.exp(jax.random.uniform(amp_key, (REPLICAS,), jnp.float32, -0.5, 0.5))
    column_sign = jnp.where(jax.random.bernoulli(column_key, 0.5, (D,)), 1.0, -1.0).astype(jnp.float32)
    column_size = jax.random.uniform(size_key, (D,), jnp.float32, 0.5, 1.5)
    offset = odd_column * column_sign * column_size * jnp.sqrt(24.0 / D)
    ramp = 0.4 * jnp.exp(place * 1.609438)
    values = jax.random.normal(noise_key, (REPLICAS, POOL, D), jnp.float32)
    spread = odd_column * 0.3 + (1.0 - odd_column) * ramp
    shifted = (replica_sign * replica_amp)[:, None, None] * offset[None, None, :]
    return jnp.clip(shifted + values * spread[None, None, :], -6.0, 6.0).astype(jnp.bfloat16)


def draw_targets(key, part):
    key = jax.random.fold_in(key, 23)
    sign_key, size_key, noise_key = jax.random.split(key, 3)
    columns = BLOCKS * FF
    column_sign = jnp.where(jax.random.bernoulli(sign_key, 0.5, (columns,)), 1.0, -1.0).astype(jnp.float32)
    column_bias = column_sign * jax.random.uniform(size_key, (columns,), jnp.float32, 0.3, 0.8)
    shape = (REPLICAS, EXP_LOCAL, STEPS * ROWS, columns)
    noise = 0.3 * jax.random.normal(noise_key, shape, jnp.float32)
    return jnp.clip(column_bias[None, None, None, :] + noise, -2.0, 2.0).astype(jnp.bfloat16)


def place_ends(values, stream_key, smallest, high):
    extent = values.shape
    index_at = [jax.random.randint(jax.random.fold_in(stream_key, axis), (), 0, extent[axis]) for axis in range(len(extent))]
    values = values.at[tuple(index_at)].set(smallest)
    longest = extent.index(max(extent))
    index_at[longest] = (index_at[longest] + 1) % extent[longest]
    return values.at[tuple(index_at)].set(high)


def block_levels(own_key, dims, cuts, least, largest):
    level, own = 1.0, jax.random.fold_in(own_key, 6)
    for position, parts in cuts:
        draws = jnp.exp(jax.random.uniform(jax.random.fold_in(own, position), (parts,), jnp.float32, least / len(cuts), largest / len(cuts)))
        level = level * jnp.repeat(draws, dims[position] // parts).reshape([-1 if axis == position else 1 for axis in range(len(dims))])
    return level


def centred(own_key, shape, scale, limit, cuts=(), kind=jnp.bfloat16):
    gain = block_levels(own_key, shape, cuts, -0.22, 0.18) if cuts else 1.0
    values = jax.random.normal(own_key, shape, jnp.float32) * scale * gain
    return jnp.minimum(jnp.maximum(values, -limit), limit).astype(kind)


def setup_inputs(seed: int = 0) -> dict:
    streams_of = jax.random.split(jax.random.key(seed), 5)
    return {
        "token_pool": draw_token_pool(jax.random.fold_in(streams_of[4], 71), 0),
        "row_index": place_ends(jax.random.randint(streams_of[1], (REPLICAS, BLOCKS, EXP_LOCAL, STEPS * ROWS), 0, POOL), jax.random.fold_in(streams_of[1], 1), 0, POOL - 1).astype(jnp.int32),
        "weights": centred(streams_of[2], (EXP_LOCAL, D, BLOCKS * FF), 1.0, 4.0, ((2, 16),)),
        "targets": draw_targets(jax.random.fold_in(streams_of[4], 71), 0),
    }


LEARN_RATE = 0.3
MOMENTUM = 0.9
EPSILON = 1e-06

def local_steps(pool_rows, indices, goals, start_weights):
    running = start_weights.astype(jnp.float32)
    velocity = jnp.zeros_like(running)
    inv_width = 1.0 / math.sqrt(pool_rows.shape[1])
    batch_rows = indices.shape[0] // STEPS
    inv_batch = 1.0 / math.sqrt(batch_rows)
    for step_index in range(STEPS):
        picked = indices[step_index * batch_rows:(step_index + 1) * batch_rows]
        inputs = jnp.take(pool_rows, picked, axis=0)
        wanted = goals[step_index * batch_rows:(step_index + 1) * batch_rows].astype(jnp.float32)
        hidden = jnp.dot(inputs, running.astype(jnp.bfloat16), preferred_element_type=jnp.float32) * inv_width
        sigma = jax.nn.sigmoid(hidden)
        slope = sigma * (1.0 + hidden * (1.0 - sigma))
        grad_hidden = ((hidden * sigma - wanted) * slope).astype(jnp.bfloat16)
        gradient = jnp.dot(inputs.T, grad_hidden, preferred_element_type=jnp.float32) * inv_batch
        velocity = MOMENTUM * velocity + gradient
        running = running - LEARN_RATE * velocity
    return (running - start_weights.astype(jnp.float32)).astype(jnp.bfloat16)

def adasum_tree(deltas):
    current = deltas.astype(jnp.float32)
    for level_index in range(LEVELS):
        pair_count = current.shape[0] // 2
        paired = current.reshape((pair_count, 2) + current.shape[1:])
        left_wide = paired[:, 0]
        right_wide = paired[:, 1]
        cross = lax.optimization_barrier(jnp.sum(left_wide * right_wide, axis=(1, 2)))
        left_square = lax.optimization_barrier(jnp.sum(left_wide * left_wide, axis=(1, 2)))
        right_square = lax.optimization_barrier(jnp.sum(right_wide * right_wide, axis=(1, 2)))
        left_coef = 1.0 - cross / (2.0 * (left_square + EPSILON))
        right_coef = 1.0 - cross / (2.0 * (right_square + EPSILON))
        current = left_coef[:, None, None] * left_wide + right_coef[:, None, None] * right_wide
    return current[0].astype(jnp.bfloat16)

def reference(token_pool, row_index, weights, targets):
    per_slot = []
    for expert_slot in range(EXP_LOCAL):
        block_parts = []
        for block_index in range(BLOCKS):
            start_weights = weights[expert_slot, :, block_index * FF:(block_index + 1) * FF]
            goals = targets[:, expert_slot, :, block_index * FF:(block_index + 1) * FF]
            deltas = jax.vmap(local_steps, in_axes=(0, 0, 0, None))(token_pool, row_index[:, block_index, expert_slot], goals, start_weights)
            combined = adasum_tree(deltas)
            block_parts.append((start_weights.astype(jnp.float32) + combined.astype(jnp.float32)).astype(jnp.bfloat16))
        per_slot.append(jnp.concatenate(block_parts, axis=1))
    return jnp.stack(per_slot, 0)
```

```python
import functools
import math

import jax
import jax.numpy as jnp
from jax import lax
from jax.experimental import pallas as pl
from jax.experimental.pallas import tpu as pltpu
from jax.sharding import PartitionSpec as P

STEPS = 4
CUT = 2
RING = 8

LEARN_RATE = 0.3
MOMENTUM = 0.9
EPSILON = 1e-06

MESH = pl.DeviceIdType.MESH
F32 = jnp.float32
BF16 = jnp.bfloat16
A_ROWS = 48


def dot(a, b):
    return jnp.dot(a, b, preferred_element_type=F32)


def dot_last(a, b):
    return lax.dot_general(a, b, (((1,), (1,)), ((), ())), preferred_element_type=F32)


def dot_first(a, b):
    return lax.dot_general(a, b, (((0,), (0,)), ((), ())), preferred_element_type=F32)


def local_steps(pool, start, picked, goals):
    pool_count, width = pool.shape
    total = picked.shape[1]
    rows = total // STEPS
    inv_width = 1.0 / math.sqrt(width)
    scale = LEARN_RATE / math.sqrt(rows)
    first = dot(pool, start)
    kernel_matrix = dot_last(pool, pool).astype(BF16)
    slots = lax.broadcasted_iota(jnp.int32, (pool_count, total), 0)
    marks = (slots == picked).astype(BF16)
    z = first
    velocity = None
    moved = None
    for step in range(STEPS):
        mark = marks[:, step * rows : (step + 1) * rows]
        high = z.astype(BF16)
        low = (z - high.astype(F32)).astype(BF16)
        hidden = (dot_first(mark, high) + dot_first(mark, low)) * inv_width
        sigma = jax.nn.sigmoid(hidden)
        slope = sigma * (1.0 + hidden * (1.0 - sigma))
        wanted = goals[step * rows : (step + 1) * rows].astype(F32)
        grad_hidden = ((hidden * sigma - wanted) * slope).astype(BF16)
        spread = dot(mark, grad_hidden)
        velocity = spread if velocity is None else MOMENTUM * velocity + spread
        moved = velocity if moved is None else moved + velocity
        if step < STEPS - 1:
            z = first - scale * dot(kernel_matrix, moved.astype(BF16))
    return (-scale * moved).astype(BF16)


def tree_coefs(gram):
    count, lanes = gram.shape
    row = lax.broadcasted_iota(jnp.int32, gram.shape, 0)
    lane = lax.broadcasted_iota(jnp.int32, gram.shape, 1)
    own = row == lane
    coef = jnp.ones((count, 1), F32)
    bit = 1
    while bit < count:
        partner = lane == (row ^ bit)
        squares = jnp.where(own, gram, 0.0)
        crosses = jnp.where(partner, gram, 0.0)
        gains = []
        for axis in (1, 0):
            square = jnp.maximum(jnp.sum(squares, axis=axis, keepdims=True), 0.0)
            cross = jnp.sum(crosses, axis=axis, keepdims=True)
            gains.append(1.0 - cross / (2.0 * (square + EPSILON)))
        coef = coef * gains[0]
        gram = gram * gains[0] * gains[1]
        gram = gram + jnp.where(
            (lane & bit) == 0, pltpu.roll(gram, lanes - bit, 1), pltpu.roll(gram, bit, 1)
        )
        gram = gram + jnp.where(
            (row & bit) == 0, pltpu.roll(gram, count - bit, 0), pltpu.roll(gram, bit, 0)
        )
        bit *= 2
    return coef


def kernel(
    pool_ref,
    index_ref,
    start_ref,
    goal_ref,
    out_ref,
    turned,
    delta,
    recv,
    wide,
    gram_pad,
    gram_one,
    gram_two,
    coefs,
    a2a_send,
    a2a_recv,
    one_send,
    one_recv,
    two_send,
    two_recv,
    ya_send,
    ya_recv,
    xa_send,
    xa_recv,
    xb_send,
    xb_recv,
    yb_send,
    yb_recv,
):
    reps = recv.shape[0]
    seg = recv.shape[1]
    cols = recv.shape[2]
    tall = reps // RING
    me = lax.axis_index("rep")
    shard = lax.axis_index("shard")
    x = me // RING
    y = me % RING
    core = shard % CUT

    barrier = pltpu.get_barrier_semaphore()

    def greet(k, carry):
        pl.semaphore_signal(
            barrier,
            inc=1,
            device_id={"rep": lax.rem(me + k, reps), "shard": shard},
            device_id_type=MESH,
        )
        return carry

    def greet_other(k, carry):
        pl.semaphore_signal(
            barrier,
            inc=1,
            device_id={"rep": x * RING + lax.rem(y + k, RING), "shard": shard ^ 1},
            device_id_type=MESH,
        )
        return carry

    lax.fori_loop(1, reps, greet, 0)
    lax.fori_loop(0, RING, greet_other, 0)

    pool = pool_ref[0]
    turned[...] = pool.T
    picked = index_ref[0, pl.ds(shard // CUT, 1), 0, :]
    weights = local_steps(pool, start_ref[0], picked, goal_ref[0, 0])

    pl.semaphore_wait(barrier, reps - 1 + RING)

    def a2a(peer):
        return pltpu.make_async_remote_copy(
            src_ref=delta.at[pl.ds(pl.multiple_of(peer * seg, seg), seg), :],
            dst_ref=recv.at[me],
            send_sem=a2a_send.at[peer],
            recv_sem=a2a_recv.at[me],
            device_id={"rep": peer, "shard": shard},
            device_id_type=MESH,
        )

    def a2a_arrival(peer):
        return pltpu.make_async_remote_copy(
            src_ref=delta.at[pl.ds(0, seg), :],
            dst_ref=recv.at[peer],
            send_sem=a2a_send.at[peer],
            recv_sem=a2a_recv.at[peer],
            device_id={"rep": peer, "shard": shard},
            device_id_type=MESH,
        )

    for i in range(tall):
        to_x = lax.rem(x + i, tall)
        base = pl.multiple_of(to_x * RING * seg, RING * seg)
        block = pl.ds(base, RING * seg)
        delta[block, :] = dot(turned[block, :], weights).astype(BF16)

        def send(j, carry, to_x=to_x):
            a2a(to_x * RING + lax.rem(y + j, RING)).start()
            return carry

        lax.fori_loop(1 if i == 0 else 0, RING, send, 0)
    recv[me] = delta[pl.ds(pl.multiple_of(me * seg, seg), seg), :]

    def arrive(k, carry):
        a2a_arrival(lax.rem(me + k, reps)).wait_recv()
        return carry

    lax.fori_loop(1, reps, arrive, 0)

    def widen(q, carry):
        for h in range(cols // 128):
            wide[h, pl.ds(pl.multiple_of(q * seg, seg), seg), :] = recv[
                q, :, 128 * h : 128 * h + 128
            ].astype(F32)
        return carry

    lax.fori_loop(0, reps, widen, 0)

    def add_row(r, total):
        for h in range(cols // 128):
            parts = wide[h, pl.ds(r, reps, stride=seg), :].astype(BF16)
            total = total + dot_last(parts, parts)
        return total

    gram = lax.fori_loop(0, seg, add_row, jnp.zeros((reps, reps), F32))
    gram_pad[...] = jnp.zeros_like(gram_pad)
    gram_pad[:, 0:reps] = gram
    packed = gram_pad[0:8, :]
    for k in range(1, reps // 8):
        packed = packed + pltpu.roll(gram_pad[8 * k : 8 * k + 8, :], reps * k, 1)

    mine = y * CUT + core
    gram_one[mine] = packed

    def one(k, arriving):
        peer = lax.rem(mine + k, RING * CUT)
        place = peer if arriving else mine
        return pltpu.make_async_remote_copy(
            src_ref=gram_one.at[mine],
            dst_ref=gram_one.at[place],
            send_sem=one_send.at[peer],
            recv_sem=one_recv.at[place],
            device_id={
                "rep": x * RING + peer // CUT,
                "shard": (shard // CUT) * CUT + peer % CUT,
            },
            device_id_type=MESH,
        )

    def one_start(k, carry):
        one(k, False).start()
        return carry

    def one_wait(k, carry):
        one(k, True).wait_recv()
        return carry

    lax.fori_loop(1, RING * CUT, one_start, 0)
    lax.fori_loop(1, RING * CUT, one_wait, 0)
    gram_two[x] = jnp.sum(gram_one[...], axis=0)

    def x_peer(i):
        return lax.rem(x + i, tall)

    def copy(src, dst, send_sem, recv_sem, rep):
        return pltpu.make_async_remote_copy(
            src_ref=src,
            dst_ref=dst,
            send_sem=send_sem,
            recv_sem=recv_sem,
            device_id={"rep": rep, "shard": shard},
            device_id_type=MESH,
        )

    for i in range(1, tall):
        p = x_peer(i)
        copy(gram_two.at[x], gram_two.at[x], two_send.at[p], two_recv.at[x], p * RING + y).start()
    for i in range(1, tall):
        p = x_peer(i)
        copy(gram_two.at[x], gram_two.at[p], two_send.at[p], two_recv.at[p], p * RING + y).wait_recv()
    packed = jnp.sum(gram_two[...], axis=0)
    lane = lax.broadcasted_iota(jnp.int32, packed.shape, 1)
    pieces = [
        jnp.where(lane < reps, packed if k == 0 else pltpu.roll(packed, 128 - reps * k, 1), 0.0)
        for k in range(reps // 8)
    ]
    gram_pad[...] = jnp.concatenate(pieces, axis=0)
    coefs[...] = jnp.broadcast_to(tree_coefs(gram_pad[...]), coefs.shape)

    def combine(q, total):
        return total + coefs[pl.ds(q, 1), :] * recv[q].astype(F32)

    combined = lax.fori_loop(0, reps, combine, jnp.zeros((seg, cols), F32)).astype(BF16)
    before = start_ref[0, pl.ds(pl.multiple_of(me * seg, seg), seg), :]
    out_ref[x, y] = (before.astype(F32) + combined.astype(F32)).astype(BF16)

    top = pl.ds(0, A_ROWS)
    low = pl.ds(A_ROWS, seg - A_ROWS)

    def y_peer(j):
        return lax.rem(y + j, RING)

    def ya(j, arriving):
        p = y_peer(j)
        return copy(
            out_ref.at[x, y, top],
            out_ref.at[x, p if arriving else y, top],
            ya_send.at[p],
            ya_recv.at[p if arriving else y],
            x * RING + p,
        )

    def xa(i, arriving):
        p = x_peer(i)
        return copy(
            out_ref.at[x, :, top],
            out_ref.at[p if arriving else x, :, top],
            xa_send.at[p],
            xa_recv.at[p if arriving else x],
            p * RING + y,
        )

    def xb(i, arriving):
        p = x_peer(i)
        return copy(
            out_ref.at[x, y, low],
            out_ref.at[p if arriving else x, y, low],
            xb_send.at[p],
            xb_recv.at[p if arriving else x],
            p * RING + y,
        )

    def yb(j, arriving):
        p = y_peer(j)
        return copy(
            out_ref.at[:, y, low],
            out_ref.at[:, p if arriving else y, low],
            yb_send.at[p],
            yb_recv.at[p if arriving else y],
            x * RING + p,
        )

    for i in range(1, tall):
        xb(i, False).start()
    for j in range(1, RING):
        ya(j, False).start()
    for i in range(1, tall):
        xb(i, True).wait_recv()
    for j in range(1, RING):
        yb(j, False).start()
    for j in range(1, RING):
        ya(j, True).wait_recv()
    for i in range(1, tall):
        xa(i, False).start()
    for j in range(1, RING):
        yb(j, True).wait_recv()
    for i in range(1, tall):
        xa(i, True).wait_recv()

    def a2a_left(k, carry):
        a2a(lax.rem(me + k, reps)).wait_send()
        return carry

    def one_left(k, carry):
        one(k, False).wait_send()
        return carry

    lax.fori_loop(1, reps, a2a_left, 0)
    lax.fori_loop(1, RING * CUT, one_left, 0)
    for i in range(1, tall):
        p = x_peer(i)
        copy(gram_two.at[x], gram_two.at[x], two_send.at[p], two_recv.at[x], p * RING + y).wait_send()
        xa(i, False).wait_send()
        xb(i, False).wait_send()
    for j in range(1, RING):
        ya(j, False).wait_send()
        yb(j, False).wait_send()


def body(token_pool, row_index, weights, targets):
    reps = lax.axis_size("rep")
    tall = reps // RING
    pool_count, width = token_pool.shape[1:]
    cols = weights.shape[2]
    seg = width // reps
    dma = pltpu.SemaphoreType.DMA
    out = pl.pallas_call(
        kernel,
        out_shape=jax.ShapeDtypeStruct((tall, RING, seg, cols), BF16),
        in_specs=[pl.BlockSpec(memory_space=pltpu.VMEM)] * 4,
        out_specs=pl.BlockSpec(memory_space=pltpu.VMEM),
        scratch_shapes=[
            pltpu.VMEM((width, pool_count), BF16),
            pltpu.VMEM((width, cols), BF16),
            pltpu.VMEM((reps, seg, cols), BF16),
            pltpu.VMEM((cols // 128, reps * seg, 128), F32),
            pltpu.VMEM((reps, 128), F32),
            pltpu.VMEM((RING * CUT, 8, 128), F32),
            pltpu.VMEM((tall, 8, 128), F32),
            pltpu.VMEM((reps, cols), F32),
            dma((reps,)),
            dma((reps,)),
            dma((RING * CUT,)),
            dma((RING * CUT,)),
            dma((tall,)),
            dma((tall,)),
            dma((RING,)),
            dma((RING,)),
            dma((tall,)),
            dma((tall,)),
            dma((tall,)),
            dma((tall,)),
            dma((RING,)),
            dma((RING,)),
        ],
        compiler_params=pltpu.CompilerParams(
            collective_id=0, has_side_effects=True, vmem_limit_bytes=40 * 1024 * 1024
        ),
    )(token_pool, row_index, weights, targets)
    return out.reshape(weights.shape)


def solution(mesh):
    in_specs = (
        P("rep", None, None),
        P("rep", None, None, None),
        P(None, None, "shard"),
        P("rep", None, None, "shard"),
    )
    out_specs = P(None, None, "shard")
    return jax.shard_map(body, mesh=mesh, in_specs=in_specs, out_specs=out_specs, check_vma=False)
```

```python
import functools
import math

import jax
import jax.numpy as jnp
from jax import lax
from jax.experimental import pallas as pl
from jax.experimental.pallas import tpu as pltpu
from jax.sharding import PartitionSpec as P

STEPS = 4
CUT = 2
RING = 8

LEARN_RATE = 0.3
MOMENTUM = 0.9
EPSILON = 1e-06

MESH = pl.DeviceIdType.MESH
F32 = jnp.float32
BF16 = jnp.bfloat16
A_ROWS = 48


def dot(a, b):
    return jnp.dot(a, b, preferred_element_type=F32)


def dot_last(a, b):
    return lax.dot_general(a, b, (((1,), (1,)), ((), ())), preferred_element_type=F32)


def dot_first(a, b):
    return lax.dot_general(a, b, (((0,), (0,)), ((), ())), preferred_element_type=F32)


def local_steps(pool, start, picked, goals):
    pool_count, width = pool.shape
    total = picked.shape[1]
    rows = total // STEPS
    inv_width = 1.0 / math.sqrt(width)
    scale = LEARN_RATE / math.sqrt(rows)
    first = dot(pool, start)
    kernel_matrix = dot_last(pool, pool).astype(BF16)
    slots = lax.broadcasted_iota(jnp.int32, (pool_count, total), 0)
    marks = (slots == picked).astype(BF16)
    z = first
    velocity = None
    moved = None
    for step in range(STEPS):
        mark = marks[:, step * rows : (step + 1) * rows]
        high = z.astype(BF16)
        low = (z - high.astype(F32)).astype(BF16)
        hidden = (dot_first(mark, high) + dot_first(mark, low)) * inv_width
        sigma = jax.nn.sigmoid(hidden)
        slope = sigma * (1.0 + hidden * (1.0 - sigma))
        wanted = goals[step * rows : (step + 1) * rows].astype(F32)
        grad_hidden = ((hidden * sigma - wanted) * slope).astype(BF16)
        spread = dot(mark, grad_hidden)
        velocity = spread if velocity is None else MOMENTUM * velocity + spread
        moved = velocity if moved is None else moved + velocity
        if step < STEPS - 1:
            z = first - scale * dot(kernel_matrix, moved.astype(BF16))
    return (-scale * moved).astype(BF16)


def tree_coefs(gram):
    count, lanes = gram.shape
    row = lax.broadcasted_iota(jnp.int32, gram.shape, 0)
    lane = lax.broadcasted_iota(jnp.int32, gram.shape, 1)
    own = row == lane
    coef = jnp.ones((count, 1), F32)
    bit = 1
    while bit < count:
        partner = lane == (row ^ bit)
        squares = jnp.where(own, gram, 0.0)
        crosses = jnp.where(partner, gram, 0.0)
        gains = []
        for axis in (1, 0):
            square = jnp.maximum(jnp.sum(squares, axis=axis, keepdims=True), 0.0)
            cross = jnp.sum(crosses, axis=axis, keepdims=True)
            gains.append(1.0 - cross / (2.0 * (square + EPSILON)))
        coef = coef * gains[0]
        gram = gram * gains[0] * gains[1]
        gram = gram + jnp.where(
            (lane & bit) == 0, pltpu.roll(gram, lanes - bit, 1), pltpu.roll(gram, bit, 1)
        )
        gram = gram + jnp.where(
            (row & bit) == 0, pltpu.roll(gram, count - bit, 0), pltpu.roll(gram, bit, 0)
        )
        bit *= 2
    return coef


def kernel(
    pool_hbm,
    index_hbm,
    start_hbm,
    goal_hbm,
    out_ref,
    pool_ref,
    index_ref,
    start_ref,
    goal_ref,
    turned,
    delta,
    recv,
    wide,
    operand,
    gram_pad,
    gram_one,
    gram_two,
    coefs,
    load_sem,
    a2a_send,
    a2a_recv,
    one_send,
    one_recv,
    two_send,
    two_recv,
    ya_send,
    ya_recv,
    xa_send,
    xa_recv,
    xb_send,
    xb_recv,
    yb_send,
    yb_recv,
):
    halves, reps, half, cols = recv.shape
    seg = halves * half
    tall = reps // RING
    pairs = tall * CUT
    me = lax.axis_index("rep")
    shard = lax.axis_index("shard")
    x = me // RING
    y = me % RING
    core = shard % CUT

    loads = [
        pltpu.make_async_copy(src, dst, load_sem.at[k])
        for k, (src, dst) in enumerate(
            (
                (pool_hbm.at[0], pool_ref),
                (start_hbm.at[0], start_ref),
                (index_hbm.at[0, pl.ds(shard // CUT, 1), 0], index_ref),
                (goal_hbm.at[0, 0], goal_ref),
            )
        )
    ]
    for load in loads:
        load.start()

    barrier = pltpu.get_barrier_semaphore()

    def greet(k, carry):
        pl.semaphore_signal(
            barrier,
            inc=1,
            device_id={"rep": lax.rem(me + k, reps), "shard": shard},
            device_id_type=MESH,
        )
        return carry

    def greet_other(i, carry):
        pl.semaphore_signal(
            barrier,
            inc=1,
            device_id={"rep": lax.rem(x + i, tall) * RING + y, "shard": shard ^ 1},
            device_id_type=MESH,
        )
        return carry

    lax.fori_loop(1, reps, greet, 0)
    lax.fori_loop(0, tall, greet_other, 0)

    def copy(src, dst, send_sem, recv_sem, rep, to_shard=None):
        return pltpu.make_async_remote_copy(
            src_ref=src,
            dst_ref=dst,
            send_sem=send_sem,
            recv_sem=recv_sem,
            device_id={"rep": rep, "shard": shard if to_shard is None else to_shard},
            device_id_type=MESH,
        )

    def x_peer(i):
        return lax.rem(x + i, tall)

    def y_peer(j):
        return lax.rem(y + j, RING)

    loads[0].wait()
    turned[...] = pool_ref[...].T
    for load in loads[1:]:
        load.wait()
    weights = local_steps(pool_ref[...], start_ref[...], index_ref[...], goal_ref[...])

    pl.semaphore_wait(barrier, reps - 1 + tall)

    def a2a(peer, h):
        return copy(
            delta.at[pl.ds(pl.multiple_of(peer * seg + h * half, half), half), :],
            recv.at[h, me],
            a2a_send.at[0],
            a2a_recv.at[h],
            peer,
        )

    def a2a_all(h):
        count = reps - 1
        return copy(
            recv.at[h, pl.ds(0, count)],
            recv.at[h, pl.ds(0, count)],
            a2a_send.at[0],
            a2a_recv.at[h],
            lax.rem(me + 1, reps),
        )

    for i in range(tall):
        to_x = x_peer(i)
        block = pl.ds(pl.multiple_of(to_x * RING * seg, RING * seg), RING * seg)
        delta[block, :] = dot(turned[block, :], weights).astype(BF16)

        def send(j, carry, to_x=to_x):
            a2a(to_x * RING + y_peer(j), 0).start()
            return carry

        lax.fori_loop(1 if i == 0 else 0, RING, send, 0)

    def send_rest(k, carry):
        a2a(lax.rem(me + k, reps), 1).start()
        return carry

    lax.fori_loop(1, reps, send_rest, 0)
    for h in range(halves):
        own = pl.ds(pl.multiple_of(me * seg + h * half, half), half)
        recv[h, me] = delta[own, :]

    gram = None
    for h in range(halves):
        a2a_all(h).wait_recv()
        for q in range(reps):
            for c in range(cols // 128):
                wide[c, half * q : half * q + half, :] = recv[
                    h, q, :, 128 * c : 128 * c + 128
                ].astype(F32)
        for r in range(half):
            for c in range(cols // 128):
                part = wide[c, pl.ds(r, reps, stride=half), :]
                place = r * cols + 128 * c
                operand[:, place : place + 128] = part.astype(BF16)
        term = dot_last(operand[...], operand[...])
        gram = term if gram is None else gram + term

    gram_pad[...] = jnp.zeros_like(gram_pad)
    gram_pad[:, 0:reps] = gram
    packed = gram_pad[0:8, :]
    for k in range(1, reps // 8):
        packed = packed + pltpu.roll(gram_pad[8 * k : 8 * k + 8, :], reps * k, 1)

    mine = x * CUT + core
    gram_one[mine] = packed

    def one(k, arriving):
        peer = lax.rem(mine + k, pairs)
        place = peer if arriving else mine
        return copy(
            gram_one.at[mine],
            gram_one.at[place],
            one_send.at[peer],
            one_recv.at[place],
            (peer // CUT) * RING + y,
            (shard // CUT) * CUT + peer % CUT,
        )

    def two(j, arriving):
        p = y_peer(j)
        place = p if arriving else y
        return copy(
            gram_two.at[y], gram_two.at[place], two_send.at[p], two_recv.at[place], x * RING + p
        )

    far_first = (4, 3, 5, 2, 6, 1, 7)
    for k in range(1, pairs):
        one(k, False).start()
    for k in range(1, pairs):
        one(k, True).wait_recv()
    gram_two[y] = jnp.sum(gram_one[...], axis=0)
    for j in far_first:
        two(j, False).start()
    for j in range(1, RING):
        two(j, True).wait_recv()
    packed = jnp.sum(gram_two[...], axis=0)
    lane = lax.broadcasted_iota(jnp.int32, packed.shape, 1)
    pieces = [
        jnp.where(lane < reps, packed if k == 0 else pltpu.roll(packed, 128 - reps * k, 1), 0.0)
        for k in range(reps // 8)
    ]
    coef = tree_coefs(jnp.concatenate(pieces, axis=0))
    coefs[...] = jnp.broadcast_to(coef, coefs.shape)

    for h in range(halves):
        total = jnp.zeros((half, cols), F32)
        for q in range(reps):
            total = total + coefs[q : q + 1, :] * recv[h, q].astype(F32)
        rows = pl.ds(pl.multiple_of(me * seg + h * half, half), half)
        combined = total.astype(BF16).astype(F32)
        out_ref[x, y, half * h : half * h + half] = (
            start_ref[rows, :].astype(F32) + combined
        ).astype(BF16)

    top = pl.ds(0, A_ROWS)
    low = pl.ds(A_ROWS, seg - A_ROWS)

    def ya(j, arriving):
        p = y_peer(j)
        place = p if arriving else y
        return copy(
            out_ref.at[x, y, top],
            out_ref.at[x, place, top],
            ya_send.at[p],
            ya_recv.at[place],
            x * RING + p,
        )

    def xa(i, j):
        p = x_peer(i)
        chunk = out_ref.at[x, y_peer(j), top]
        return copy(chunk, chunk, xa_send.at[p], xa_recv.at[x], p * RING + y)

    def xa_all(i):
        p = x_peer(i)
        return copy(
            out_ref.at[x, :, top], out_ref.at[p, :, top], xa_send.at[p], xa_recv.at[p], p * RING + y
        )

    def xb(i, arriving):
        p = x_peer(i)
        place = p if arriving else x
        return copy(
            out_ref.at[x, y, low],
            out_ref.at[place, y, low],
            xb_send.at[p],
            xb_recv.at[place],
            p * RING + y,
        )

    def yb(j, arriving):
        p = y_peer(j)
        place = p if arriving else y
        return copy(
            out_ref.at[:, y, low],
            out_ref.at[:, place, low],
            yb_send.at[p],
            yb_recv.at[place],
            x * RING + p,
        )

    near_first = (1, 7, 2, 6, 3, 5, 4)
    across = (2, 1, 3)
    for i in across:
        xb(i, False).start()
    for j in near_first:
        ya(j, False).start()
    for i in across:
        xa(i, 0).start()
    for i in range(1, tall):
        xb(i, True).wait_recv()
    for j in far_first:
        yb(j, False).start()
    for j in near_first:
        ya(j, True).wait_recv()
        for i in across:
            xa(i, j).start()
    for j in range(1, RING):
        yb(j, True).wait_recv()
    for i in range(1, tall):
        xa_all(i).wait_recv()

    for h in range(halves):
        a2a_all(h).wait_send()
    for k in range(1, pairs):
        one(k, False).wait_send()
    for j in range(1, RING):
        two(j, False).wait_send()
        ya(j, False).wait_send()
        yb(j, False).wait_send()
    for i in range(1, tall):
        xa_all(i).wait_send()
        xb(i, False).wait_send()


def body(token_pool, row_index, weights, targets):
    reps = lax.axis_size("rep")
    tall = reps // RING
    pool_count, width = token_pool.shape[1:]
    total = row_index.shape[3]
    cols = weights.shape[2]
    seg = width // reps
    half = seg // 2
    dma = pltpu.SemaphoreType.DMA
    out = pl.pallas_call(
        kernel,
        out_shape=jax.ShapeDtypeStruct((tall, RING, seg, cols), BF16),
        in_specs=[pl.BlockSpec(memory_space=pltpu.HBM)] * 4,
        out_specs=pl.BlockSpec(memory_space=pltpu.VMEM),
        scratch_shapes=[
            pltpu.VMEM((pool_count, width), BF16),
            pltpu.VMEM((1, total), jnp.int32),
            pltpu.VMEM((width, cols), BF16),
            pltpu.VMEM((total, cols), BF16),
            pltpu.VMEM((width, pool_count), BF16),
            pltpu.VMEM((width, cols), BF16),
            pltpu.VMEM((2, reps, half, cols), BF16),
            pltpu.VMEM((cols // 128, reps * half, 128), F32),
            pltpu.VMEM((reps, half * cols), BF16),
            pltpu.VMEM((reps, 128), F32),
            pltpu.VMEM((tall * CUT, 8, 128), F32),
            pltpu.VMEM((RING, 8, 128), F32),
            pltpu.VMEM((reps, cols), F32),
            dma((4,)),
            dma((1,)),
            dma((2,)),
            dma((tall * CUT,)),
            dma((tall * CUT,)),
            dma((RING,)),
            dma((RING,)),
            dma((RING,)),
            dma((RING,)),
            dma((tall,)),
            dma((tall,)),
            dma((tall,)),
            dma((tall,)),
            dma((RING,)),
            dma((RING,)),
        ],
        compiler_params=pltpu.CompilerParams(
            collective_id=0, has_side_effects=True, vmem_limit_bytes=60 * 1024 * 1024
        ),
    )(token_pool, row_index, weights, targets)
    return out.reshape(weights.shape)


def solution(mesh):
    in_specs = (
        P("rep", None, None),
        P("rep", None, None, None),
        P(None, None, "shard"),
        P("rep", None, None, "shard"),
    )
    out_specs = P(None, None, "shard")
    return jax.shard_map(body, mesh=mesh, in_specs=in_specs, out_specs=out_specs, check_vma=False)
```

```python
import functools
import math

import jax
import jax.numpy as jnp
from jax import lax
from jax.experimental import pallas as pl
from jax.experimental.pallas import tpu as pltpu
from jax.sharding import PartitionSpec as P

STEPS = 4
CUT = 2
RING = 8

LEARN_RATE = 0.3
MOMENTUM = 0.9
EPSILON = 1e-06

MESH = pl.DeviceIdType.MESH
F32 = jnp.float32
BF16 = jnp.bfloat16
PARTS = (48, 16)


def hops(place):
    i, j = place
    return min(i, 4 - i) + min(j, RING - j)


OTHERS = sorted(((i, j) for i in range(4) for j in range(RING) if i or j), key=hops, reverse=True)


def dot(a, b):
    return jnp.dot(a, b, preferred_element_type=F32)


def dot_last(a, b):
    return lax.dot_general(a, b, (((1,), (1,)), ((), ())), preferred_element_type=F32)


def dot_first(a, b):
    return lax.dot_general(a, b, (((0,), (0,)), ((), ())), preferred_element_type=F32)


def local_steps(pool, start, picked, goals):
    pool_count, width = pool.shape
    total = picked.shape[1]
    rows = total // STEPS
    inv_width = 1.0 / math.sqrt(width)
    scale = LEARN_RATE / math.sqrt(rows)
    first = dot(pool, start)
    kernel_matrix = dot_last(pool, pool).astype(BF16)
    slots = lax.broadcasted_iota(jnp.int32, (pool_count, total), 0)
    marks = (slots == picked).astype(BF16)
    z = first
    velocity = None
    moved = None
    for step in range(STEPS):
        mark = marks[:, step * rows : (step + 1) * rows]
        high = z.astype(BF16)
        low = (z - high.astype(F32)).astype(BF16)
        hidden = (dot_first(mark, high) + dot_first(mark, low)) * inv_width
        sigma = jax.nn.sigmoid(hidden)
        slope = sigma * (1.0 + hidden * (1.0 - sigma))
        wanted = goals[step * rows : (step + 1) * rows].astype(F32)
        grad_hidden = ((hidden * sigma - wanted) * slope).astype(BF16)
        spread = dot(mark, grad_hidden)
        velocity = spread if velocity is None else MOMENTUM * velocity + spread
        moved = velocity if moved is None else moved + velocity
        if step < STEPS - 1:
            z = first - scale * dot(kernel_matrix, moved.astype(BF16))
    return (-scale * moved).astype(BF16)


def tree_coefs(gram):
    count, lanes = gram.shape
    row = lax.broadcasted_iota(jnp.int32, gram.shape, 0)
    lane = lax.broadcasted_iota(jnp.int32, gram.shape, 1)
    own = row == lane
    coef = jnp.ones((count, 1), F32)
    bit = 1
    while bit < count:
        partner = lane == (row ^ bit)
        squares = jnp.where(own, gram, 0.0)
        crosses = jnp.where(partner, gram, 0.0)
        gains = []
        for axis in (1, 0):
            square = jnp.maximum(jnp.sum(squares, axis=axis, keepdims=True), 0.0)
            cross = jnp.sum(crosses, axis=axis, keepdims=True)
            gains.append(1.0 - cross / (2.0 * (square + EPSILON)))
        coef = coef * gains[0]
        gram = gram * gains[0] * gains[1]
        gram = gram + jnp.where(
            (lane & bit) == 0, pltpu.roll(gram, lanes - bit, 1), pltpu.roll(gram, bit, 1)
        )
        gram = gram + jnp.where(
            (row & bit) == 0, pltpu.roll(gram, count - bit, 0), pltpu.roll(gram, bit, 0)
        )
        bit *= 2
    return coef


def kernel(
    pool_hbm,
    index_hbm,
    start_hbm,
    goal_hbm,
    out_ref,
    pool_ref,
    index_ref,
    start_ref,
    goal_ref,
    turned,
    delta,
    recv_top,
    recv_low,
    wide,
    operand,
    gram_pad,
    gram_core,
    gram_all,
    coefs,
    load_sem,
    a2a_send,
    a2a_recv,
    one_send,
    one_recv,
    two_send,
    two_recv,
    ya_send,
    ya_recv,
    xa_send,
    xa_recv,
    xb_send,
    xb_recv,
    yb_send,
    yb_recv,
):
    reps, _, cols = recv_top.shape
    recv = (recv_top, recv_low)
    starts = (0, PARTS[0])
    seg = sum(PARTS)
    tall = reps // RING
    me = lax.axis_index("rep")
    shard = lax.axis_index("shard")
    x = me // RING
    y = me % RING
    core = shard % CUT

    loads = [
        pltpu.make_async_copy(src, dst, load_sem.at[k])
        for k, (src, dst) in enumerate(
            (
                (pool_hbm.at[0], pool_ref),
                (start_hbm.at[0], start_ref),
                (index_hbm.at[0, pl.ds(shard // CUT, 1), 0], index_ref),
                (goal_hbm.at[0, 0], goal_ref),
            )
        )
    ]
    for load in loads:
        load.start()

    barrier = pltpu.get_barrier_semaphore()

    def x_peer(i):
        return lax.rem(x + i, tall)

    def y_peer(j):
        return lax.rem(y + j, RING)

    def peer_at(place):
        return x_peer(place[0]) * RING + y_peer(place[1])

    for place in OTHERS:
        pl.semaphore_signal(
            barrier,
            inc=1,
            device_id={"rep": peer_at(place), "shard": shard},
            device_id_type=MESH,
        )
    pl.semaphore_signal(
        barrier, inc=1, device_id={"rep": me, "shard": shard ^ 1}, device_id_type=MESH
    )

    def copy(src, dst, send_sem, recv_sem, rep, to_shard=None):
        return pltpu.make_async_remote_copy(
            src_ref=src,
            dst_ref=dst,
            send_sem=send_sem,
            recv_sem=recv_sem,
            device_id={"rep": rep, "shard": shard if to_shard is None else to_shard},
            device_id_type=MESH,
        )

    loads[0].wait()
    turned[...] = pool_ref[...].T
    for load in loads[1:]:
        load.wait()
    weights = local_steps(pool_ref[...], start_ref[...], index_ref[...], goal_ref[...])

    pl.semaphore_wait(barrier, reps)

    def a2a(peer, h):
        return copy(
            delta.at[pl.ds(pl.multiple_of(peer * seg + starts[h], 16), PARTS[h]), :],
            recv[h].at[me],
            a2a_send.at[0],
            a2a_recv.at[h],
            peer,
        )

    def a2a_all(h):
        count = reps - 1
        return copy(
            recv[h].at[pl.ds(0, count)],
            recv[h].at[pl.ds(0, count)],
            a2a_send.at[0],
            a2a_recv.at[h],
            lax.rem(me + 1, reps),
        )

    order = (4, 1, 7, 3, 5, 2, 6, 0)
    for h in range(len(PARTS)):
        for i in (2, 1, 3, 0):
            if h == 0:
                block = pl.ds(pl.multiple_of(x_peer(i) * RING * seg, RING * seg), RING * seg)
                delta[block, :] = dot(turned[block, :], weights).astype(BF16)
            for j in order:
                if i or j:
                    a2a(peer_at((i, j)), h).start()

    def own(h):
        return pl.ds(pl.multiple_of(me * seg + starts[h], 16), PARTS[h])

    gram = None
    for h, rows in enumerate(PARTS):
        recv[h][me] = delta[own(h), :]
        a2a_all(h).wait_recv()
        for q in range(reps):
            for c in range(cols // 128):
                wide[c, rows * q : rows * q + rows, :] = recv[h][
                    q, :, 128 * c : 128 * c + 128
                ].astype(F32)
        for r in range(rows):
            for c in range(cols // 128):
                part = wide[c, pl.ds(r, reps, stride=rows), :]
                place = r * cols + 128 * c
                operand[:, place : place + 128] = part.astype(BF16)
        sides = operand[:, 0 : rows * cols]
        term = dot_last(sides, sides)
        gram = term if gram is None else gram + term

    gram_pad[...] = jnp.zeros_like(gram_pad)
    gram_pad[:, 0:reps] = gram
    packed = gram_pad[0:8, :]
    for k in range(1, reps // 8):
        packed = packed + pltpu.roll(gram_pad[8 * k : 8 * k + 8, :], reps * k, 1)

    gram_core[core] = packed

    def one(place):
        return copy(
            gram_core.at[core],
            gram_core.at[place],
            one_send.at[0],
            one_recv.at[0],
            me,
            shard ^ 1,
        )

    def two(place):
        return copy(
            gram_all.at[me], gram_all.at[me], two_send.at[0], two_recv.at[0], peer_at(place)
        )

    def two_all():
        every = gram_all.at[pl.ds(0, reps - 1)]
        return copy(every, every, two_send.at[0], two_recv.at[0], peer_at(OTHERS[0]))

    one(core).start()
    one(1 - core).wait_recv()
    gram_all[me] = gram_core[0] + gram_core[1]
    for place in OTHERS:
        two(place).start()
    two_all().wait_recv()
    packed = jnp.sum(gram_all[...], axis=0)
    lane = lax.broadcasted_iota(jnp.int32, packed.shape, 1)
    pieces = [
        jnp.where(lane < reps, packed if k == 0 else pltpu.roll(packed, 128 - reps * k, 1), 0.0)
        for k in range(reps // 8)
    ]
    coef = tree_coefs(jnp.concatenate(pieces, axis=0))
    coefs[...] = jnp.broadcast_to(coef, coefs.shape)

    def finish(h):
        total = jnp.zeros((PARTS[h], cols), F32)
        for q in range(reps):
            total = total + coefs[q : q + 1, :] * recv[h][q].astype(F32)
        combined = total.astype(BF16).astype(F32)
        out_ref[x, y, starts[h] : starts[h] + PARTS[h]] = (
            start_ref[own(h), :].astype(F32) + combined
        ).astype(BF16)

    top = pl.ds(0, PARTS[0])
    low = pl.ds(PARTS[0], PARTS[1])

    def ya(j, arriving):
        p = y_peer(j)
        place = p if arriving else y
        return copy(
            out_ref.at[x, y, top],
            out_ref.at[x, place, top],
            ya_send.at[p],
            ya_recv.at[place],
            x * RING + p,
        )

    def xa(i, j):
        p = x_peer(i)
        chunk = out_ref.at[x, y_peer(j), top]
        return copy(chunk, chunk, xa_send.at[p], xa_recv.at[x], p * RING + y)

    def xa_all(i):
        p = x_peer(i)
        return copy(
            out_ref.at[x, :, top], out_ref.at[p, :, top], xa_send.at[p], xa_recv.at[p], p * RING + y
        )

    def xb(i, arriving):
        p = x_peer(i)
        place = p if arriving else x
        return copy(
            out_ref.at[x, y, low],
            out_ref.at[place, y, low],
            xb_send.at[p],
            xb_recv.at[place],
            p * RING + y,
        )

    def yb(j, arriving):
        p = y_peer(j)
        place = p if arriving else y
        return copy(
            out_ref.at[:, y, low],
            out_ref.at[:, place, low],
            yb_send.at[p],
            yb_recv.at[place],
            x * RING + p,
        )

    near_first = (1, 7, 2, 6, 3, 5, 4)
    far_first = (4, 3, 5, 2, 6, 1, 7)
    across = (2, 1, 3)
    finish(1)
    for i in across:
        xb(i, False).start()
    finish(0)
    for j in near_first:
        ya(j, False).start()
    for i in across:
        xa(i, 0).start()
    for i in range(1, tall):
        xb(i, True).wait_recv()
    for j in far_first:
        yb(j, False).start()
    for j in near_first:
        ya(j, True).wait_recv()
        for i in across:
            xa(i, j).start()
    for j in range(1, RING):
        yb(j, True).wait_recv()
    for i in range(1, tall):
        xa_all(i).wait_recv()

    for h in range(len(PARTS)):
        a2a_all(h).wait_send()
    one(core).wait_send()
    two_all().wait_send()
    for j in range(1, RING):
        ya(j, False).wait_send()
        yb(j, False).wait_send()
    for i in range(1, tall):
        xa_all(i).wait_send()
        xb(i, False).wait_send()


def body(token_pool, row_index, weights, targets):
    reps = lax.axis_size("rep")
    tall = reps // RING
    pool_count, width = token_pool.shape[1:]
    total = row_index.shape[3]
    cols = weights.shape[2]
    seg = width // reps
    dma = pltpu.SemaphoreType.DMA
    out = pl.pallas_call(
        kernel,
        out_shape=jax.ShapeDtypeStruct((tall, RING, seg, cols), BF16),
        in_specs=[pl.BlockSpec(memory_space=pltpu.HBM)] * 4,
        out_specs=pl.BlockSpec(memory_space=pltpu.VMEM),
        scratch_shapes=[
            pltpu.VMEM((pool_count, width), BF16),
            pltpu.VMEM((1, total), jnp.int32),
            pltpu.VMEM((width, cols), BF16),
            pltpu.VMEM((total, cols), BF16),
            pltpu.VMEM((width, pool_count), BF16),
            pltpu.VMEM((width, cols), BF16),
            pltpu.VMEM((reps, PARTS[0], cols), BF16),
            pltpu.VMEM((reps, PARTS[1], cols), BF16),
            pltpu.VMEM((cols // 128, reps * PARTS[0], 128), F32),
            pltpu.VMEM((reps, PARTS[0] * cols), BF16),
            pltpu.VMEM((reps, 128), F32),
            pltpu.VMEM((CUT, 8, 128), F32),
            pltpu.VMEM((reps, 8, 128), F32),
            pltpu.VMEM((reps, cols), F32),
            dma((4,)),
            dma((1,)),
            dma((2,)),
            dma((1,)),
            dma((1,)),
            dma((1,)),
            dma((1,)),
            dma((RING,)),
            dma((RING,)),
            dma((tall,)),
            dma((tall,)),
            dma((tall,)),
            dma((tall,)),
            dma((RING,)),
            dma((RING,)),
        ],
        compiler_params=pltpu.CompilerParams(
            collective_id=0, has_side_effects=True, vmem_limit_bytes=40 * 1024 * 1024
        ),
    )(
        *(
            pltpu.with_memory_space_constraint(array, pltpu.HBM)
            for array in (token_pool, row_index, weights, targets)
        )
    )
    return out.reshape(weights.shape)


def solution(mesh):
    in_specs = (
        P("rep", None, None),
        P("rep", None, None, None),
        P(None, None, "shard"),
        P("rep", None, None, "shard"),
    )
    out_specs = P(None, None, "shard")
    return jax.shard_map(body, mesh=mesh, in_specs=in_specs, out_specs=out_specs, check_vma=False)
```

```python
import functools
import math

import jax
import jax.numpy as jnp
from jax import lax
from jax.experimental import pallas as pl
from jax.experimental.pallas import tpu as pltpu
from jax.sharding import PartitionSpec as P

STEPS = 4
CUT = 2
RING = 8

LEARN_RATE = 0.3
MOMENTUM = 0.9
EPSILON = 1e-06

MESH = pl.DeviceIdType.MESH
F32 = jnp.float32
BF16 = jnp.bfloat16
PARTS = (48, 16)
LOADS = 4


def hops(place):
    i, j = place
    return min(i, 4 - i) + min(j, RING - j)


OTHERS = sorted(((i, j) for i in range(4) for j in range(RING) if i or j), key=hops, reverse=True)


def dot(a, b):
    return jnp.dot(a, b, preferred_element_type=F32)


def dot_last(a, b):
    return lax.dot_general(a, b, (((1,), (1,)), ((), ())), preferred_element_type=F32)


def dot_first(a, b):
    return lax.dot_general(a, b, (((0,), (0,)), ((), ())), preferred_element_type=F32)


def routing(picked, pool_count):
    slots = lax.broadcasted_iota(jnp.int32, (pool_count, picked.shape[1]), 0)
    marks = jnp.where(slots == picked, 1.0, 0.0)
    return marks.astype(BF16), marks.T.astype(BF16)


def local_steps(first, products, marks, picks, goals, width, gates):
    rows = marks.shape[1] // STEPS
    inv_width = 1.0 / math.sqrt(width)
    scale = LEARN_RATE / math.sqrt(rows)
    reach = [sum(MOMENTUM**k for k in range(n)) for n in range(STEPS + 1)]
    high = first.astype(BF16)
    low = (first - high.astype(F32)).astype(BF16)
    base = (dot(picks, high) + dot(picks, low)) * inv_width
    routed = dot(picks[rows:], products.astype(BF16)).astype(BF16)
    moved = None
    for step in range(STEPS):
        block = slice(step * rows, (step + 1) * rows)
        hidden = base[block]
        if step:
            met = dot(routed[(step - 1) * rows : step * rows], marks[:, 0 : step * rows])
            parts = [
                met[:, s * rows : (s + 1) * rows] * (-scale * inv_width * reach[step - s])
                for s in range(step)
            ]
            met = jnp.concatenate(parts, axis=1).astype(BF16)
            hidden = hidden + dot(met, gates[0 : step * rows, :])
        sigma = jax.nn.sigmoid(hidden)
        slope = sigma * (1.0 + hidden * (1.0 - sigma))
        wanted = goals[block].astype(F32)
        grad_hidden = ((hidden * sigma - wanted) * slope).astype(BF16)
        gates[block, :] = grad_hidden
        term = dot(marks[:, block], grad_hidden) * (-scale * reach[STEPS - step])
        moved = term if moved is None else moved + term
    return moved.astype(BF16)


def tree_coefs(gram):
    count, lanes = gram.shape
    row = lax.broadcasted_iota(jnp.int32, gram.shape, 0)
    lane = lax.broadcasted_iota(jnp.int32, gram.shape, 1)
    own = row == lane
    coef = jnp.ones((count, 1), F32)
    bit = 1
    while bit < count:
        partner = lane == (row ^ bit)
        squares = jnp.where(own, gram, 0.0)
        crosses = jnp.where(partner, gram, 0.0)
        gains = []
        for axis in (1, 0):
            square = jnp.maximum(jnp.sum(squares, axis=axis, keepdims=True), 0.0)
            cross = jnp.sum(crosses, axis=axis, keepdims=True)
            gains.append(1.0 - cross / (2.0 * (square + EPSILON)))
        coef = coef * gains[0]
        gram = gram * gains[0] * gains[1]
        gram = gram + jnp.where(
            (lane & bit) == 0, pltpu.roll(gram, lanes - bit, 1), pltpu.roll(gram, bit, 1)
        )
        gram = gram + jnp.where(
            (row & bit) == 0, pltpu.roll(gram, count - bit, 0), pltpu.roll(gram, bit, 0)
        )
        bit *= 2
    return coef


def kernel(
    pool_hbm,
    index_hbm,
    start_hbm,
    goal_hbm,
    out_ref,
    pool_ref,
    index_ref,
    start_ref,
    goal_ref,
    gates,
    turned,
    delta,
    recv_top,
    recv_low,
    wide,
    operand,
    gram_pad,
    gram_core,
    gram_all,
    coefs,
    load_sem,
    a2a_send,
    a2a_recv,
    one_send,
    one_recv,
    two_send,
    two_recv,
    ya_send,
    ya_recv,
    xa_send,
    xa_recv,
    xb_send,
    xb_recv,
    yb_send,
    yb_recv,
):
    reps, _, cols = recv_top.shape
    recv = (recv_top, recv_low)
    starts = (0, PARTS[0])
    seg = sum(PARTS)
    tall = reps // RING
    me = lax.axis_index("rep")
    shard = lax.axis_index("shard")
    x = me // RING
    y = me % RING
    core = shard % CUT

    pool_count, width = pool_ref.shape
    span = width // LOADS

    def load(src, dst, k):
        started = pltpu.make_async_copy(src, dst, load_sem.at[k])
        started.start()
        return started

    index_load = load(index_hbm.at[0, pl.ds(shard // CUT, 1), 0], index_ref, 0)
    loads = []
    for k in range(LOADS):
        part = pl.ds(k * span, span)
        loads.append(
            (
                load(pool_hbm.at[0, :, part], pool_ref.at[:, part], 2 + 2 * k),
                load(start_hbm.at[0, part], start_ref.at[part], 3 + 2 * k),
            )
        )
    goal_load = load(goal_hbm.at[0, 0], goal_ref, 1)

    barrier = pltpu.get_barrier_semaphore()

    def x_peer(i):
        return lax.rem(x + i, tall)

    def y_peer(j):
        return lax.rem(y + j, RING)

    def peer_at(place):
        return x_peer(place[0]) * RING + y_peer(place[1])

    for place in OTHERS:
        pl.semaphore_signal(
            barrier,
            inc=1,
            device_id={"rep": peer_at(place), "shard": shard},
            device_id_type=MESH,
        )
    pl.semaphore_signal(
        barrier, inc=1, device_id={"rep": me, "shard": shard ^ 1}, device_id_type=MESH
    )

    def copy(src, dst, send_sem, recv_sem, rep, to_shard=None):
        return pltpu.make_async_remote_copy(
            src_ref=src,
            dst_ref=dst,
            send_sem=send_sem,
            recv_sem=recv_sem,
            device_id={"rep": rep, "shard": shard if to_shard is None else to_shard},
            device_id_type=MESH,
        )

    index_load.wait()
    marks, picks = routing(index_ref[...], pool_count)
    first = products = None
    for k in range(LOADS):
        for part in loads[k]:
            part.wait()
        tokens = pool_ref[:, k * span : (k + 1) * span]
        turned[k * span : (k + 1) * span, :] = tokens.T
        one_first = dot(tokens, start_ref[k * span : (k + 1) * span, :])
        one_products = dot_last(tokens, tokens)
        first = one_first if first is None else first + one_first
        products = one_products if products is None else products + one_products
    goal_load.wait()
    weights = local_steps(first, products, marks, picks, goal_ref, width, gates)

    pl.semaphore_wait(barrier, reps)

    def a2a(peer, h):
        return copy(
            delta.at[pl.ds(pl.multiple_of(peer * seg + starts[h], 16), PARTS[h]), :],
            recv[h].at[me],
            a2a_send.at[0],
            a2a_recv.at[h],
            peer,
        )

    def a2a_all(h):
        count = reps - 1
        return copy(
            recv[h].at[pl.ds(0, count)],
            recv[h].at[pl.ds(0, count)],
            a2a_send.at[0],
            a2a_recv.at[h],
            lax.rem(me + 1, reps),
        )

    order = (4, 1, 7, 3, 5, 2, 6, 0)
    for h in range(len(PARTS)):
        for i in (2, 1, 3, 0):
            if h == 0:
                block = pl.ds(pl.multiple_of(x_peer(i) * RING * seg, RING * seg), RING * seg)
                delta[block, :] = dot(turned[block, :], weights).astype(BF16)
            for j in order:
                if i or j:
                    a2a(peer_at((i, j)), h).start()

    def own(h):
        return pl.ds(pl.multiple_of(me * seg + starts[h], 16), PARTS[h])

    gram = None
    for h, rows in enumerate(PARTS):
        recv[h][me] = delta[own(h), :]
        a2a_all(h).wait_recv()
        for q in range(reps):
            for c in range(cols // 128):
                wide[c, rows * q : rows * q + rows, :] = recv[h][
                    q, :, 128 * c : 128 * c + 128
                ].astype(F32)
        for r in range(rows):
            for c in range(cols // 128):
                part = wide[c, pl.ds(r, reps, stride=rows), :]
                place = r * cols + 128 * c
                operand[:, place : place + 128] = part.astype(BF16)
        sides = operand[:, 0 : rows * cols]
        term = dot_last(sides, sides)
        gram = term if gram is None else gram + term

    gram_pad[...] = jnp.zeros_like(gram_pad)
    gram_pad[:, 0:reps] = gram
    packed = gram_pad[0:8, :]
    for k in range(1, reps // 8):
        packed = packed + pltpu.roll(gram_pad[8 * k : 8 * k + 8, :], reps * k, 1)

    gram_core[core] = packed

    def one(place):
        return copy(
            gram_core.at[core],
            gram_core.at[place],
            one_send.at[0],
            one_recv.at[0],
            me,
            shard ^ 1,
        )

    def two(place):
        return copy(
            gram_all.at[me], gram_all.at[me], two_send.at[0], two_recv.at[0], peer_at(place)
        )

    def two_all():
        every = gram_all.at[pl.ds(0, reps - 1)]
        return copy(every, every, two_send.at[0], two_recv.at[0], peer_at(OTHERS[0]))

    one(core).start()
    one(1 - core).wait_recv()
    gram_all[me] = gram_core[0] + gram_core[1]
    for place in OTHERS:
        two(place).start()
    two_all().wait_recv()
    packed = jnp.sum(gram_all[...], axis=0)
    lane = lax.broadcasted_iota(jnp.int32, packed.shape, 1)
    pieces = [
        jnp.where(lane < reps, packed if k == 0 else pltpu.roll(packed, 128 - reps * k, 1), 0.0)
        for k in range(reps // 8)
    ]
    coef = tree_coefs(jnp.concatenate(pieces, axis=0))
    coefs[...] = jnp.broadcast_to(coef, coefs.shape)

    def finish(h):
        total = jnp.zeros((PARTS[h], cols), F32)
        for q in range(reps):
            total = total + coefs[q : q + 1, :] * recv[h][q].astype(F32)
        combined = total.astype(BF16).astype(F32)
        out_ref[x, y, starts[h] : starts[h] + PARTS[h]] = (
            start_ref[own(h), :].astype(F32) + combined
        ).astype(BF16)

    top = pl.ds(0, PARTS[0])
    low = pl.ds(PARTS[0], PARTS[1])

    def ya(j, arriving):
        p = y_peer(j)
        place = p if arriving else y
        return copy(
            out_ref.at[x, y, top],
            out_ref.at[x, place, top],
            ya_send.at[p],
            ya_recv.at[place],
            x * RING + p,
        )

    def xa(i, j):
        p = x_peer(i)
        chunk = out_ref.at[x, y_peer(j), top]
        return copy(chunk, chunk, xa_send.at[p], xa_recv.at[x], p * RING + y)

    def xa_all(i):
        p = x_peer(i)
        return copy(
            out_ref.at[x, :, top], out_ref.at[p, :, top], xa_send.at[p], xa_recv.at[p], p * RING + y
        )

    def xb(i, arriving):
        p = x_peer(i)
        place = p if arriving else x
        return copy(
            out_ref.at[x, y, low],
            out_ref.at[place, y, low],
            xb_send.at[p],
            xb_recv.at[place],
            p * RING + y,
        )

    def yb(j, arriving):
        p = y_peer(j)
        place = p if arriving else y
        return copy(
            out_ref.at[:, y, low],
            out_ref.at[:, place, low],
            yb_send.at[p],
            yb_recv.at[place],
            x * RING + p,
        )

    near_first = (1, 7, 2, 6, 3, 5, 4)
    far_first = (4, 3, 5, 2, 6, 1, 7)
    across = (2, 1, 3)
    finish(1)
    for i in across:
        xb(i, False).start()
    finish(0)
    for j in near_first:
        ya(j, False).start()
    for i in across:
        xa(i, 0).start()
    for i in range(1, tall):
        xb(i, True).wait_recv()
    for j in far_first:
        yb(j, False).start()
    for j in near_first:
        ya(j, True).wait_recv()
        for i in across:
            xa(i, j).start()
    for j in range(1, RING):
        yb(j, True).wait_recv()
    for i in range(1, tall):
        xa_all(i).wait_recv()

    for h in range(len(PARTS)):
        a2a_all(h).wait_send()
    one(core).wait_send()
    two_all().wait_send()
    for j in range(1, RING):
        ya(j, False).wait_send()
        yb(j, False).wait_send()
    for i in range(1, tall):
        xa_all(i).wait_send()
        xb(i, False).wait_send()


def body(token_pool, row_index, weights, targets):
    reps = lax.axis_size("rep")
    tall = reps // RING
    pool_count, width = token_pool.shape[1:]
    total = row_index.shape[3]
    cols = weights.shape[2]
    seg = width // reps
    dma = pltpu.SemaphoreType.DMA
    out = pl.pallas_call(
        kernel,
        out_shape=jax.ShapeDtypeStruct((tall, RING, seg, cols), BF16),
        in_specs=[pl.BlockSpec(memory_space=pltpu.HBM)] * 4,
        out_specs=pl.BlockSpec(memory_space=pltpu.VMEM),
        scratch_shapes=[
            pltpu.VMEM((pool_count, width), BF16),
            pltpu.VMEM((1, total), jnp.int32),
            pltpu.VMEM((width, cols), BF16),
            pltpu.VMEM((total, cols), BF16),
            pltpu.VMEM((total, cols), BF16),
            pltpu.VMEM((width, pool_count), BF16),
            pltpu.VMEM((width, cols), BF16),
            pltpu.VMEM((reps, PARTS[0], cols), BF16),
            pltpu.VMEM((reps, PARTS[1], cols), BF16),
            pltpu.VMEM((cols // 128, reps * PARTS[0], 128), F32),
            pltpu.VMEM((reps, PARTS[0] * cols), BF16),
            pltpu.VMEM((reps, 128), F32),
            pltpu.VMEM((CUT, 8, 128), F32),
            pltpu.VMEM((reps, 8, 128), F32),
            pltpu.VMEM((reps, cols), F32),
            dma((2 + 2 * LOADS,)),
            dma((1,)),
            dma((2,)),
            dma((1,)),
            dma((1,)),
            dma((1,)),
            dma((1,)),
            dma((RING,)),
            dma((RING,)),
            dma((tall,)),
            dma((tall,)),
            dma((tall,)),
            dma((tall,)),
            dma((RING,)),
            dma((RING,)),
        ],
        compiler_params=pltpu.CompilerParams(
            collective_id=0, has_side_effects=True, vmem_limit_bytes=40 * 1024 * 1024
        ),
    )(
        *(
            pltpu.with_memory_space_constraint(array, pltpu.HBM)
            for array in (token_pool, row_index, weights, targets)
        )
    )
    return out.reshape(weights.shape)


def solution(mesh):
    in_specs = (
        P("rep", None, None),
        P("rep", None, None, None),
        P(None, None, "shard"),
        P("rep", None, None, "shard"),
    )
    out_specs = P(None, None, "shard")
    return jax.shard_map(body, mesh=mesh, in_specs=in_specs, out_specs=out_specs, check_vma=False)
```

```python
import functools
import math

import jax
import jax.numpy as jnp
from jax import lax
from jax.experimental import pallas as pl
from jax.experimental.pallas import tpu as pltpu
from jax.sharding import PartitionSpec as P

STEPS = 4
CUT = 2
RING = 8

LEARN_RATE = 0.3
MOMENTUM = 0.9
EPSILON = 1e-06

MESH = pl.DeviceIdType.MESH
F32 = jnp.float32
BF16 = jnp.bfloat16
PARTS = (48, 16)
FORWARD = 6
LOADS = 4


def hops(place):
    i, j = place
    return min(i, 4 - i) + min(j, RING - j)


OTHERS = sorted(((i, j) for i in range(4) for j in range(RING) if i or j), key=hops, reverse=True)


def dot(a, b):
    return jnp.dot(a, b, preferred_element_type=F32)


def dot_last(a, b):
    return lax.dot_general(a, b, (((1,), (1,)), ((), ())), preferred_element_type=F32)


def dot_first(a, b):
    return lax.dot_general(a, b, (((0,), (0,)), ((), ())), preferred_element_type=F32)


def routing(picked, pool_count):
    slots = lax.broadcasted_iota(jnp.int32, (pool_count, picked.shape[1]), 0)
    marks = jnp.where(slots == picked, 1.0, 0.0)
    return marks.astype(BF16), marks.T.astype(BF16)


def local_steps(first, products, marks, picks, goals, width, gates):
    rows = marks.shape[1] // STEPS
    inv_width = 1.0 / math.sqrt(width)
    scale = LEARN_RATE / math.sqrt(rows)
    reach = [sum(MOMENTUM**k for k in range(n)) for n in range(STEPS + 1)]
    high = first.astype(BF16)
    low = (first - high.astype(F32)).astype(BF16)
    base = (dot(picks, high) + dot(picks, low)) * inv_width
    routed = dot(picks[rows:], products.astype(BF16)).astype(BF16)
    moved = None
    for step in range(STEPS):
        block = slice(step * rows, (step + 1) * rows)
        hidden = base[block]
        if step:
            met = dot(routed[(step - 1) * rows : step * rows], marks[:, 0 : step * rows])
            parts = [
                met[:, s * rows : (s + 1) * rows] * (-scale * inv_width * reach[step - s])
                for s in range(step)
            ]
            met = jnp.concatenate(parts, axis=1).astype(BF16)
            hidden = hidden + dot(met, gates[0 : step * rows, :])
        sigma = jax.nn.sigmoid(hidden)
        slope = sigma * (1.0 + hidden * (1.0 - sigma))
        wanted = goals[block].astype(F32)
        grad_hidden = ((hidden * sigma - wanted) * slope).astype(BF16)
        gates[block, :] = grad_hidden
        term = dot(marks[:, block], grad_hidden) * (-scale * reach[STEPS - step])
        moved = term if moved is None else moved + term
    return moved.astype(BF16)


def tree_coefs(gram):
    count, lanes = gram.shape
    row = lax.broadcasted_iota(jnp.int32, gram.shape, 0)
    lane = lax.broadcasted_iota(jnp.int32, gram.shape, 1)
    own = row == lane
    coef = jnp.ones((count, 1), F32)
    bit = 1
    while bit < count:
        partner = lane == (row ^ bit)
        squares = jnp.where(own, gram, 0.0)
        crosses = jnp.where(partner, gram, 0.0)
        gains = []
        for axis in (1, 0):
            square = jnp.maximum(jnp.sum(squares, axis=axis, keepdims=True), 0.0)
            cross = jnp.sum(crosses, axis=axis, keepdims=True)
            gains.append(1.0 - cross / (2.0 * (square + EPSILON)))
        coef = coef * gains[0]
        gram = gram * gains[0] * gains[1]
        gram = gram + jnp.where(
            (lane & bit) == 0, pltpu.roll(gram, lanes - bit, 1), pltpu.roll(gram, bit, 1)
        )
        gram = gram + jnp.where(
            (row & bit) == 0, pltpu.roll(gram, count - bit, 0), pltpu.roll(gram, bit, 0)
        )
        bit *= 2
    return coef


def kernel(
    pool_hbm,
    index_hbm,
    start_hbm,
    goal_hbm,
    out_ref,
    pool_ref,
    index_ref,
    start_ref,
    goal_ref,
    gates,
    turned,
    delta,
    recv_top,
    recv_low,
    wide,
    operand,
    gram_pad,
    gram_core,
    gram_all,
    coefs,
    load_sem,
    a2a_send,
    a2a_recv,
    one_send,
    one_recv,
    two_send,
    two_recv,
    ya_send,
    ya_recv,
    xa_send,
    xa_recv,
    xb_send,
    xb_recv,
    yb_send,
    yb_recv,
):
    reps, _, cols = recv_top.shape
    recv = (recv_top, recv_low)
    starts = (0, PARTS[0])
    seg = sum(PARTS)
    tall = reps // RING
    me = lax.axis_index("rep")
    shard = lax.axis_index("shard")
    x = me // RING
    y = me % RING
    core = shard % CUT

    pool_count, width = pool_ref.shape
    span = width // LOADS

    def load(src, dst, k):
        started = pltpu.make_async_copy(src, dst, load_sem.at[k])
        started.start()
        return started

    index_load = load(index_hbm.at[0, pl.ds(shard // CUT, 1), 0], index_ref, 0)
    loads = []
    for k in range(LOADS):
        part = pl.ds(k * span, span)
        loads.append(
            (
                load(pool_hbm.at[0, :, part], pool_ref.at[:, part], 2 + 2 * k),
                load(start_hbm.at[0, part], start_ref.at[part], 3 + 2 * k),
            )
        )
    goal_load = load(goal_hbm.at[0, 0], goal_ref, 1)

    barrier = pltpu.get_barrier_semaphore()

    def x_peer(i):
        return lax.rem(x + i, tall)

    def y_peer(j):
        return lax.rem(y + j, RING)

    def peer_at(place):
        return x_peer(place[0]) * RING + y_peer(place[1])

    for place in OTHERS:
        pl.semaphore_signal(
            barrier,
            inc=1,
            device_id={"rep": peer_at(place), "shard": shard},
            device_id_type=MESH,
        )
    pl.semaphore_signal(
        barrier, inc=1, device_id={"rep": me, "shard": shard ^ 1}, device_id_type=MESH
    )

    def copy(src, dst, send_sem, recv_sem, rep, to_shard=None):
        return pltpu.make_async_remote_copy(
            src_ref=src,
            dst_ref=dst,
            send_sem=send_sem,
            recv_sem=recv_sem,
            device_id={"rep": rep, "shard": shard if to_shard is None else to_shard},
            device_id_type=MESH,
        )

    index_load.wait()
    marks, picks = routing(index_ref[...], pool_count)
    first = products = None
    for k in range(LOADS):
        for part in loads[k]:
            part.wait()
        tokens = pool_ref[:, k * span : (k + 1) * span]
        turned[k * span : (k + 1) * span, :] = tokens.T
        one_first = dot(tokens, start_ref[k * span : (k + 1) * span, :])
        one_products = dot_last(tokens, tokens)
        first = one_first if first is None else first + one_first
        products = one_products if products is None else products + one_products
    goal_load.wait()
    weights = local_steps(first, products, marks, picks, goal_ref, width, gates)

    pl.semaphore_wait(barrier, reps)

    def a2a(peer, h):
        return copy(
            delta.at[pl.ds(pl.multiple_of(peer * seg + starts[h], 16), PARTS[h]), :],
            recv[h].at[me],
            a2a_send.at[0],
            a2a_recv.at[h],
            peer,
        )

    def a2a_all(h):
        count = reps - 1
        return copy(
            recv[h].at[pl.ds(0, count)],
            recv[h].at[pl.ds(0, count)],
            a2a_send.at[0],
            a2a_recv.at[h],
            lax.rem(me + 1, reps),
        )

    order = (4, 1, 7, 3, 5, 2, 6, 0)
    for h in range(len(PARTS)):
        for i in (2, 1, 3, 0):
            if h == 0:
                block = pl.ds(pl.multiple_of(x_peer(i) * RING * seg, RING * seg), RING * seg)
                delta[block, :] = dot(turned[block, :], weights).astype(BF16)
            for j in order:
                if i or j:
                    a2a(peer_at((i, j)), h).start()

    def own(h):
        return pl.ds(pl.multiple_of(me * seg + starts[h], 16), PARTS[h])

    gram = None
    for h, rows in enumerate(PARTS):
        recv[h][me] = delta[own(h), :]
        a2a_all(h).wait_recv()
        for q in range(reps):
            for c in range(cols // 128):
                wide[c, rows * q : rows * q + rows, :] = recv[h][
                    q, :, 128 * c : 128 * c + 128
                ].astype(F32)
        for r in range(rows):
            for c in range(cols // 128):
                part = wide[c, pl.ds(r, reps, stride=rows), :]
                place = r * cols + 128 * c
                operand[:, place : place + 128] = part.astype(BF16)
        sides = operand[:, 0 : rows * cols]
        term = dot_last(sides, sides)
        gram = term if gram is None else gram + term

    gram_pad[...] = jnp.zeros_like(gram_pad)
    gram_pad[:, 0:reps] = gram
    packed = gram_pad[0:8, :]
    for k in range(1, reps // 8):
        packed = packed + pltpu.roll(gram_pad[8 * k : 8 * k + 8, :], reps * k, 1)

    gram_core[core] = packed

    def one(place):
        return copy(
            gram_core.at[core],
            gram_core.at[place],
            one_send.at[0],
            one_recv.at[0],
            me,
            shard ^ 1,
        )

    def two(place):
        return copy(
            gram_all.at[me], gram_all.at[me], two_send.at[0], two_recv.at[0], peer_at(place)
        )

    def two_all():
        every = gram_all.at[pl.ds(0, reps - 1)]
        return copy(every, every, two_send.at[0], two_recv.at[0], peer_at(OTHERS[0]))

    one(core).start()
    one(1 - core).wait_recv()
    gram_all[me] = gram_core[0] + gram_core[1]
    for place in OTHERS:
        two(place).start()
    two_all().wait_recv()
    packed = jnp.sum(gram_all[...], axis=0)
    lane = lax.broadcasted_iota(jnp.int32, packed.shape, 1)
    pieces = [
        jnp.where(lane < reps, packed if k == 0 else pltpu.roll(packed, 128 - reps * k, 1), 0.0)
        for k in range(reps // 8)
    ]
    coef = tree_coefs(jnp.concatenate(pieces, axis=0))
    coefs[...] = jnp.broadcast_to(coef, coefs.shape)

    def finish(h):
        total = jnp.zeros((PARTS[h], cols), F32)
        for q in range(reps):
            total = total + coefs[q : q + 1, :] * recv[h][q].astype(F32)
        combined = total.astype(BF16).astype(F32)
        out_ref[x, y, starts[h] : starts[h] + PARTS[h]] = (
            start_ref[own(h), :].astype(F32) + combined
        ).astype(BF16)

    top = pl.ds(0, PARTS[0])
    low = pl.ds(PARTS[0], PARTS[1])

    def ya(j, arriving):
        p = y_peer(j)
        place = p if arriving else y
        return copy(
            out_ref.at[x, y, top],
            out_ref.at[x, place, top],
            ya_send.at[p],
            ya_recv.at[place],
            x * RING + p,
        )

    def xa(i, j):
        p = x_peer(i)
        chunk = out_ref.at[x, y_peer(j), top]
        return copy(chunk, chunk, xa_send.at[p], xa_recv.at[x], p * RING + y)

    def xa_all(i):
        p = x_peer(i)
        return copy(
            out_ref.at[x, :, top], out_ref.at[p, :, top], xa_send.at[p], xa_recv.at[p], p * RING + y
        )

    def xb(i, arriving):
        p = x_peer(i)
        place = p if arriving else x
        return copy(
            out_ref.at[x, y, low],
            out_ref.at[place, y, low],
            xb_send.at[p],
            xb_recv.at[place],
            p * RING + y,
        )

    def yb(k, to_j, from_j, some=slice(None)):
        chunk = out_ref.at[some, y_peer(from_j), low]
        place = y_peer(from_j)
        return copy(chunk, chunk, yb_send.at[k], yb_recv.at[place], x * RING + y_peer(to_j))

    def yb_hops():
        first = [yb(k, j, 0) for k, j in enumerate((2, 6, 1, 7))]
        side = tall // 2
        second = [
            yb(4, 1, 6),
            yb(5, 7, 2),
            yb(6, 2, 6, pl.ds(0, side)),
            yb(7, 6, 2, pl.ds(side, tall - side)),
        ]
        return first, second

    def yb_arrive(j):
        yb(0, j, j).wait_recv()

    near_first = (1, 7, 2, 6, 3, 5, 4)
    across = (2, 1, 3)
    finish(0)
    for j in near_first:
        ya(j, False).start()
    for i in across:
        xa(i, 0).start()
    finish(1)
    for i in across:
        xb(i, False).start()
    for n, j in enumerate(near_first):
        ya(j, True).wait_recv()
        for i in across:
            xa(i, j).start()
        if n == 1:
            for i in range(1, tall):
                xb(i, True).wait_recv()
            for hop in yb_hops()[0]:
                hop.start()
        if n == FORWARD:
            yb_arrive(6)
            yb_arrive(2)
            for hop in yb_hops()[1]:
                hop.start()
    for j in (1, 7, 3, 5, 4):
        yb_arrive(j)
    for i in range(1, tall):
        xa_all(i).wait_recv()

    for h in range(len(PARTS)):
        a2a_all(h).wait_send()
    for hops_made in yb_hops():
        for hop in hops_made:
            hop.wait_send()
    one(core).wait_send()
    two_all().wait_send()
    for j in range(1, RING):
        ya(j, False).wait_send()
    for i in range(1, tall):
        xa_all(i).wait_send()
        xb(i, False).wait_send()


def body(token_pool, row_index, weights, targets):
    reps = lax.axis_size("rep")
    tall = reps // RING
    pool_count, width = token_pool.shape[1:]
    total = row_index.shape[3]
    cols = weights.shape[2]
    seg = width // reps
    dma = pltpu.SemaphoreType.DMA
    out = pl.pallas_call(
        kernel,
        out_shape=jax.ShapeDtypeStruct((tall, RING, seg, cols), BF16),
        in_specs=[pl.BlockSpec(memory_space=pltpu.HBM)] * 4,
        out_specs=pl.BlockSpec(memory_space=pltpu.VMEM),
        scratch_shapes=[
            pltpu.VMEM((pool_count, width), BF16),
            pltpu.VMEM((1, total), jnp.int32),
            pltpu.VMEM((width, cols), BF16),
            pltpu.VMEM((total, cols), BF16),
            pltpu.VMEM((total, cols), BF16),
            pltpu.VMEM((width, pool_count), BF16),
            pltpu.VMEM((width, cols), BF16),
            pltpu.VMEM((reps, PARTS[0], cols), BF16),
            pltpu.VMEM((reps, PARTS[1], cols), BF16),
            pltpu.VMEM((cols // 128, (reps + 1) * PARTS[0], 128), F32),
            pltpu.VMEM((reps, PARTS[0] * cols), BF16),
            pltpu.VMEM((reps, 128), F32),
            pltpu.VMEM((CUT, 8, 128), F32),
            pltpu.VMEM((reps, 8, 128), F32),
            pltpu.VMEM((reps, cols), F32),
            dma((2 + 2 * LOADS,)),
            dma((1,)),
            dma((2,)),
            dma((1,)),
            dma((1,)),
            dma((1,)),
            dma((1,)),
            dma((RING,)),
            dma((RING,)),
            dma((tall,)),
            dma((tall,)),
            dma((tall,)),
            dma((tall,)),
            dma((RING,)),
            dma((RING,)),
        ],
        compiler_params=pltpu.CompilerParams(
            collective_id=0, has_side_effects=True, vmem_limit_bytes=40 * 1024 * 1024
        ),
    )(
        *(
            pltpu.with_memory_space_constraint(array, pltpu.HBM)
            for array in (token_pool, row_index, weights, targets)
        )
    )
    return out.reshape(weights.shape)


def solution(mesh):
    in_specs = (
        P("rep", None, None),
        P("rep", None, None, None),
        P(None, None, "shard"),
        P("rep", None, None, "shard"),
    )
    out_specs = P(None, None, "shard")
    return jax.shard_map(body, mesh=mesh, in_specs=in_specs, out_specs=out_specs, check_vma=False)
```

```python
import functools
import math

import jax
import jax.numpy as jnp
from jax import lax
from jax.experimental import pallas as pl
from jax.experimental.pallas import tpu as pltpu
from jax.sharding import PartitionSpec as P

STEPS = 4
CUT = 2
RING = 8

LEARN_RATE = 0.3
MOMENTUM = 0.9
EPSILON = 1e-06

MESH = pl.DeviceIdType.MESH
F32 = jnp.float32
BF16 = jnp.bfloat16
PARTS = (48, 16)
LOADS = 4


def hops(place):
    i, j = place
    return min(i, 4 - i) + min(j, RING - j)


OTHERS = sorted(((i, j) for i in range(4) for j in range(RING) if i or j), key=hops, reverse=True)


def dot(a, b):
    return jnp.dot(a, b, preferred_element_type=F32)


def dot_last(a, b):
    return lax.dot_general(a, b, (((1,), (1,)), ((), ())), preferred_element_type=F32)


def dot_first(a, b):
    return lax.dot_general(a, b, (((0,), (0,)), ((), ())), preferred_element_type=F32)


def routing(picked, pool_count):
    slots = lax.broadcasted_iota(jnp.int32, (pool_count, picked.shape[1]), 0)
    marks = jnp.where(slots == picked, 1.0, 0.0)
    return marks.astype(BF16), marks.T.astype(BF16)


def local_steps(first, products, marks, picks, goals, width, gates):
    rows = marks.shape[1] // STEPS
    inv_width = 1.0 / math.sqrt(width)
    scale = LEARN_RATE / math.sqrt(rows)
    reach = [sum(MOMENTUM**k for k in range(n)) for n in range(STEPS + 1)]
    high = first.astype(BF16)
    low = (first - high.astype(F32)).astype(BF16)
    base = (dot(picks, high) + dot(picks, low)) * inv_width
    routed = dot(picks[rows:], products.astype(BF16)).astype(BF16)
    moved = None
    for step in range(STEPS):
        block = slice(step * rows, (step + 1) * rows)
        hidden = base[block]
        if step:
            met = dot(routed[(step - 1) * rows : step * rows], marks[:, 0 : step * rows])
            parts = [
                met[:, s * rows : (s + 1) * rows] * (-scale * inv_width * reach[step - s])
                for s in range(step)
            ]
            met = jnp.concatenate(parts, axis=1).astype(BF16)
            hidden = hidden + dot(met, gates[0 : step * rows, :])
        sigma = jax.nn.sigmoid(hidden)
        slope = sigma * (1.0 + hidden * (1.0 - sigma))
        wanted = goals[block].astype(F32)
        grad_hidden = ((hidden * sigma - wanted) * slope).astype(BF16)
        gates[block, :] = grad_hidden
        term = dot(marks[:, block], grad_hidden) * (-scale * reach[STEPS - step])
        moved = term if moved is None else moved + term
    return moved.astype(BF16)


def tree_coefs(gram):
    count, lanes = gram.shape
    row = lax.broadcasted_iota(jnp.int32, gram.shape, 0)
    lane = lax.broadcasted_iota(jnp.int32, gram.shape, 1)
    own = row == lane
    coef = jnp.ones((count, 1), F32)
    bit = 1
    while bit < count:
        partner = lane == (row ^ bit)
        squares = jnp.where(own, gram, 0.0)
        crosses = jnp.where(partner, gram, 0.0)
        gains = []
        for axis in (1, 0):
            square = jnp.maximum(jnp.sum(squares, axis=axis, keepdims=True), 0.0)
            cross = jnp.sum(crosses, axis=axis, keepdims=True)
            gains.append(1.0 - cross / (2.0 * (square + EPSILON)))
        coef = coef * gains[0]
        gram = gram * gains[0] * gains[1]
        gram = gram + jnp.where(
            (lane & bit) == 0, pltpu.roll(gram, lanes - bit, 1), pltpu.roll(gram, bit, 1)
        )
        gram = gram + jnp.where(
            (row & bit) == 0, pltpu.roll(gram, count - bit, 0), pltpu.roll(gram, bit, 0)
        )
        bit *= 2
    return coef


def kernel(
    pool_hbm,
    index_hbm,
    start_hbm,
    goal_hbm,
    out_ref,
    pool_ref,
    index_ref,
    start_ref,
    goal_ref,
    gates,
    turned,
    delta,
    recv_top,
    recv_low,
    wide,
    operand,
    gram_pad,
    gram_core,
    gram_all,
    coefs,
    load_sem,
    a2a_send,
    a2a_recv,
    one_send,
    one_recv,
    two_send,
    two_recv,
    ya_send,
    ya_recv,
    xa_send,
    xa_recv,
    xb_send,
    xb_recv,
    yb_send,
    yb_recv,
):
    reps, _, cols = recv_top.shape
    recv = (recv_top, recv_low)
    starts = (0, PARTS[0])
    seg = sum(PARTS)
    tall = reps // RING
    me = lax.axis_index("rep")
    shard = lax.axis_index("shard")
    x = me // RING
    y = me % RING
    core = shard % CUT

    pool_count, width = pool_ref.shape
    span = width // LOADS

    def load(src, dst, k):
        started = pltpu.make_async_copy(src, dst, load_sem.at[k])
        started.start()
        return started

    index_load = load(index_hbm.at[0, pl.ds(shard // CUT, 1), 0], index_ref, 0)
    loads = []
    for k in range(LOADS):
        part = pl.ds(k * span, span)
        loads.append(
            (
                load(pool_hbm.at[0, :, part], pool_ref.at[:, part], 2 + 2 * k),
                load(start_hbm.at[0, part], start_ref.at[part], 3 + 2 * k),
            )
        )
    goal_load = load(goal_hbm.at[0, 0], goal_ref, 1)

    barrier = pltpu.get_barrier_semaphore()

    def x_peer(i):
        return lax.rem(x + i, tall)

    def y_peer(j):
        return lax.rem(y + j, RING)

    def peer_at(place):
        return x_peer(place[0]) * RING + y_peer(place[1])

    for place in OTHERS:
        pl.semaphore_signal(
            barrier,
            inc=1,
            device_id={"rep": peer_at(place), "shard": shard},
            device_id_type=MESH,
        )
    pl.semaphore_signal(
        barrier, inc=1, device_id={"rep": me, "shard": shard ^ 1}, device_id_type=MESH
    )

    def copy(src, dst, send_sem, recv_sem, rep, to_shard=None):
        return pltpu.make_async_remote_copy(
            src_ref=src,
            dst_ref=dst,
            send_sem=send_sem,
            recv_sem=recv_sem,
            device_id={"rep": rep, "shard": shard if to_shard is None else to_shard},
            device_id_type=MESH,
        )

    index_load.wait()
    marks, picks = routing(index_ref[...], pool_count)
    first = products = None
    for k in range(LOADS):
        for part in loads[k]:
            part.wait()
        tokens = pool_ref[:, k * span : (k + 1) * span]
        turned[k * span : (k + 1) * span, :] = tokens.T
        one_first = dot(tokens, start_ref[k * span : (k + 1) * span, :])
        one_products = dot_last(tokens, tokens)
        first = one_first if first is None else first + one_first
        products = one_products if products is None else products + one_products
    goal_load.wait()
    weights = local_steps(first, products, marks, picks, goal_ref, width, gates)

    pl.semaphore_wait(barrier, reps)

    def a2a(peer, h):
        return copy(
            delta.at[pl.ds(pl.multiple_of(peer * seg + starts[h], 16), PARTS[h]), :],
            recv[h].at[me],
            a2a_send.at[0],
            a2a_recv.at[h],
            peer,
        )

    def a2a_all(h):
        count = reps - 1
        return copy(
            recv[h].at[pl.ds(0, count)],
            recv[h].at[pl.ds(0, count)],
            a2a_send.at[0],
            a2a_recv.at[h],
            lax.rem(me + 1, reps),
        )

    order = (4, 1, 7, 3, 5, 2, 6, 0)
    for h in range(len(PARTS)):
        for i in (2, 1, 3, 0):
            if h == 0:
                block = pl.ds(pl.multiple_of(x_peer(i) * RING * seg, RING * seg), RING * seg)
                delta[block, :] = dot(turned[block, :], weights).astype(BF16)
            for j in order:
                if i or j:
                    a2a(peer_at((i, j)), h).start()

    def own(h):
        return pl.ds(pl.multiple_of(me * seg + starts[h], 16), PARTS[h])

    gram = None
    for h, rows in enumerate(PARTS):
        recv[h][me] = delta[own(h), :]
        a2a_all(h).wait_recv()
        for q in range(reps):
            for c in range(cols // 128):
                wide[c, rows * q : rows * q + rows, :] = recv[h][
                    q, :, 128 * c : 128 * c + 128
                ].astype(F32)
        for r in range(rows):
            for c in range(cols // 128):
                part = wide[c, pl.ds(r, reps, stride=rows), :]
                place = r * cols + 128 * c
                operand[:, place : place + 128] = part.astype(BF16)
        sides = operand[:, 0 : rows * cols]
        term = dot_last(sides, sides)
        gram = term if gram is None else gram + term

    gram_pad[...] = jnp.zeros_like(gram_pad)
    gram_pad[:, 0:reps] = gram
    packed = gram_pad[0:8, :]
    for k in range(1, reps // 8):
        packed = packed + pltpu.roll(gram_pad[8 * k : 8 * k + 8, :], reps * k, 1)

    gram_core[core] = packed

    def one(place):
        return copy(
            gram_core.at[core],
            gram_core.at[place],
            one_send.at[0],
            one_recv.at[0],
            me,
            shard ^ 1,
        )

    def two(place):
        return copy(
            gram_all.at[me], gram_all.at[me], two_send.at[0], two_recv.at[0], peer_at(place)
        )

    def two_all():
        every = gram_all.at[pl.ds(0, reps - 1)]
        return copy(every, every, two_send.at[0], two_recv.at[0], peer_at(OTHERS[0]))

    one(core).start()
    one(1 - core).wait_recv()
    gram_all[me] = gram_core[0] + gram_core[1]
    for place in OTHERS:
        two(place).start()
    two_all().wait_recv()
    packed = jnp.sum(gram_all[...], axis=0)
    lane = lax.broadcasted_iota(jnp.int32, packed.shape, 1)
    pieces = [
        jnp.where(lane < reps, packed if k == 0 else pltpu.roll(packed, 128 - reps * k, 1), 0.0)
        for k in range(reps // 8)
    ]
    coef = tree_coefs(jnp.concatenate(pieces, axis=0))
    coefs[...] = jnp.broadcast_to(coef, coefs.shape)

    def finish(h):
        total = jnp.zeros((PARTS[h], cols), F32)
        for q in range(reps):
            total = total + coefs[q : q + 1, :] * recv[h][q].astype(F32)
        combined = total.astype(BF16).astype(F32)
        out_ref[x, y, starts[h] : starts[h] + PARTS[h]] = (
            start_ref[own(h), :].astype(F32) + combined
        ).astype(BF16)

    top = pl.ds(0, PARTS[0])
    low = pl.ds(PARTS[0], PARTS[1])

    def ya(j, arriving):
        p = y_peer(j)
        place = p if arriving else y
        return copy(
            out_ref.at[x, y, top],
            out_ref.at[x, place, top],
            ya_send.at[p],
            ya_recv.at[place],
            x * RING + p,
        )

    def xa(i, j):
        p = x_peer(i)
        chunk = out_ref.at[x, y_peer(j), top]
        return copy(chunk, chunk, xa_send.at[p], xa_recv.at[x], p * RING + y)

    def xa_all(i):
        p = x_peer(i)
        return copy(
            out_ref.at[x, :, top], out_ref.at[p, :, top], xa_send.at[p], xa_recv.at[p], p * RING + y
        )

    def xb(i, arriving):
        p = x_peer(i)
        place = p if arriving else x
        return copy(
            out_ref.at[x, y, low],
            out_ref.at[place, y, low],
            xb_send.at[p],
            xb_recv.at[place],
            p * RING + y,
        )

    def yb(j, arriving):
        p = y_peer(j)
        place = p if arriving else y
        return copy(
            out_ref.at[:, y, low],
            out_ref.at[:, place, low],
            yb_send.at[p],
            yb_recv.at[place],
            x * RING + p,
        )

    near_first = (1, 7, 2, 6, 3, 5, 4)
    far_first = (4, 3, 5, 2, 6, 1, 7)
    across = (2, 1, 3)
    finish(1)
    for i in across:
        xb(i, False).start()
    finish(0)
    for j in near_first:
        ya(j, False).start()
    for i in across:
        xa(i, 0).start()
    for i in range(1, tall):
        xb(i, True).wait_recv()
    for j in far_first:
        yb(j, False).start()
    for j in near_first:
        ya(j, True).wait_recv()
        for i in across:
            xa(i, j).start()
    for j in range(1, RING):
        yb(j, True).wait_recv()
    for i in range(1, tall):
        xa_all(i).wait_recv()

    for h in range(len(PARTS)):
        a2a_all(h).wait_send()
    one(core).wait_send()
    two_all().wait_send()
    for j in range(1, RING):
        ya(j, False).wait_send()
        yb(j, False).wait_send()
    for i in range(1, tall):
        xa_all(i).wait_send()
        xb(i, False).wait_send()


def body(token_pool, row_index, weights, targets):
    reps = lax.axis_size("rep")
    tall = reps // RING
    pool_count, width = token_pool.shape[1:]
    total = row_index.shape[3]
    cols = weights.shape[2]
    seg = width // reps
    dma = pltpu.SemaphoreType.DMA
    out = pl.pallas_call(
        kernel,
        out_shape=jax.ShapeDtypeStruct((tall, RING, seg, cols), BF16),
        in_specs=[pl.BlockSpec(memory_space=pltpu.HBM)] * 4,
        out_specs=pl.BlockSpec(memory_space=pltpu.VMEM),
        scratch_shapes=[
            pltpu.VMEM((pool_count, width), BF16),
            pltpu.VMEM((1, total), jnp.int32),
            pltpu.VMEM((width, cols), BF16),
            pltpu.VMEM((total, cols), BF16),
            pltpu.VMEM((total, cols), BF16),
            pltpu.VMEM((width, pool_count), BF16),
            pltpu.VMEM((width, cols), BF16),
            pltpu.VMEM((reps, PARTS[0], cols), BF16),
            pltpu.VMEM((reps, PARTS[1], cols), BF16),
            pltpu.VMEM((cols // 128, (reps + 1) * PARTS[0], 128), F32),
            pltpu.VMEM((reps, PARTS[0] * cols), BF16),
            pltpu.VMEM((reps, 128), F32),
            pltpu.VMEM((CUT, 8, 128), F32),
            pltpu.VMEM((reps, 8, 128), F32),
            pltpu.VMEM((reps, cols), F32),
            dma((2 + 2 * LOADS,)),
            dma((1,)),
            dma((2,)),
            dma((1,)),
            dma((1,)),
            dma((1,)),
            dma((1,)),
            dma((RING,)),
            dma((RING,)),
            dma((tall,)),
            dma((tall,)),
            dma((tall,)),
            dma((tall,)),
            dma((RING,)),
            dma((RING,)),
        ],
        compiler_params=pltpu.CompilerParams(
            collective_id=0, has_side_effects=True, vmem_limit_bytes=40 * 1024 * 1024
        ),
    )(
        *(
            pltpu.with_memory_space_constraint(array, pltpu.HBM)
            for array in (token_pool, row_index, weights, targets)
        )
    )
    return out.reshape(weights.shape)


def solution(mesh):
    in_specs = (
        P("rep", None, None),
        P("rep", None, None, None),
        P(None, None, "shard"),
        P("rep", None, None, "shard"),
    )
    out_specs = P(None, None, "shard")
    return jax.shard_map(body, mesh=mesh, in_specs=in_specs, out_specs=out_specs, check_vma=False)
```

```python
import functools
import math

import jax
import jax.numpy as jnp
from jax import lax
from jax.experimental import pallas as pl
from jax.experimental.pallas import tpu as pltpu
from jax.sharding import PartitionSpec as P

STEPS = 4
CUT = 2
RING = 8

LEARN_RATE = 0.3
MOMENTUM = 0.9
EPSILON = 1e-06

MESH = pl.DeviceIdType.MESH
F32 = jnp.float32
BF16 = jnp.bfloat16
PARTS = (48, 16)
LOADS = 4


def hops(place):
    i, j = place
    return min(i, 4 - i) + min(j, RING - j)


OTHERS = sorted(((i, j) for i in range(4) for j in range(RING) if i or j), key=hops, reverse=True)


def dot(a, b):
    return jnp.dot(a, b, preferred_element_type=F32)


def dot_last(a, b):
    return lax.dot_general(a, b, (((1,), (1,)), ((), ())), preferred_element_type=F32)


def dot_first(a, b):
    return lax.dot_general(a, b, (((0,), (0,)), ((), ())), preferred_element_type=F32)


def routing(picked, pool_count):
    slots = lax.broadcasted_iota(jnp.int32, (pool_count, picked.shape[1]), 0)
    marks = jnp.where(slots == picked, 1.0, 0.0)
    return marks.astype(BF16), marks.T.astype(BF16)


def local_steps(first, products, marks, picks, goals, width, gates):
    rows = marks.shape[1] // STEPS
    inv_width = 1.0 / math.sqrt(width)
    scale = LEARN_RATE / math.sqrt(rows)
    reach = [sum(MOMENTUM**k for k in range(n)) for n in range(STEPS + 1)]
    high = first.astype(BF16)
    low = (first - high.astype(F32)).astype(BF16)
    base = (dot(picks, high) + dot(picks, low)) * inv_width
    routed = dot(picks[rows:], products.astype(BF16)).astype(BF16)
    moved = None
    for step in range(STEPS):
        block = slice(step * rows, (step + 1) * rows)
        hidden = base[block]
        if step:
            met = dot(routed[(step - 1) * rows : step * rows], marks[:, 0 : step * rows])
            parts = [
                met[:, s * rows : (s + 1) * rows] * (-scale * inv_width * reach[step - s])
                for s in range(step)
            ]
            met = jnp.concatenate(parts, axis=1).astype(BF16)
            hidden = hidden + dot(met, gates[0 : step * rows, :])
        sigma = jax.nn.sigmoid(hidden)
        slope = sigma * (1.0 + hidden * (1.0 - sigma))
        wanted = goals[block].astype(F32)
        grad_hidden = ((hidden * sigma - wanted) * slope).astype(BF16)
        gates[block, :] = grad_hidden
        term = dot(marks[:, block], grad_hidden) * (-scale * reach[STEPS - step])
        moved = term if moved is None else moved + term
    return moved.astype(BF16)


def tree_coefs(gram):
    count, lanes = gram.shape
    row = lax.broadcasted_iota(jnp.int32, gram.shape, 0)
    lane = lax.broadcasted_iota(jnp.int32, gram.shape, 1)
    own = row == lane
    coef = jnp.ones((count, 1), F32)
    bit = 1
    while bit < count:
        partner = lane == (row ^ bit)
        squares = jnp.where(own, gram, 0.0)
        crosses = jnp.where(partner, gram, 0.0)
        gains = []
        for axis in (1, 0):
            square = jnp.maximum(jnp.sum(squares, axis=axis, keepdims=True), 0.0)
            cross = jnp.sum(crosses, axis=axis, keepdims=True)
            gains.append(1.0 - cross / (2.0 * (square + EPSILON)))
        coef = coef * gains[0]
        gram = gram * gains[0] * gains[1]
        gram = gram + jnp.where(
            (lane & bit) == 0, pltpu.roll(gram, lanes - bit, 1), pltpu.roll(gram, bit, 1)
        )
        gram = gram + jnp.where(
            (row & bit) == 0, pltpu.roll(gram, count - bit, 0), pltpu.roll(gram, bit, 0)
        )
        bit *= 2
    return coef


def kernel(
    pool_hbm,
    index_hbm,
    start_hbm,
    goal_hbm,
    out_ref,
    pool_ref,
    index_ref,
    start_ref,
    goal_ref,
    gates,
    turned,
    delta,
    recv_top,
    recv_low,
    wide,
    operand,
    gram_pad,
    gram_core,
    gram_all,
    coefs,
    load_sem,
    a2a_send,
    a2a_recv,
    one_send,
    one_recv,
    two_send,
    two_recv,
    ya_send,
    ya_recv,
    xa_send,
    xa_recv,
    xb_send,
    xb_recv,
    yb_send,
    yb_recv,
):
    reps, _, cols = recv_top.shape
    recv = (recv_top, recv_low)
    starts = (0, PARTS[0])
    seg = sum(PARTS)
    tall = reps // RING
    me = lax.axis_index("rep")
    shard = lax.axis_index("shard")
    x = me // RING
    y = me % RING
    core = shard % CUT

    pool_count, width = pool_ref.shape
    span = width // LOADS

    def load(src, dst, k):
        started = pltpu.make_async_copy(src, dst, load_sem.at[k])
        started.start()
        return started

    index_load = load(index_hbm.at[0, pl.ds(shard // CUT, 1), 0], index_ref, 0)
    loads = []
    for k in range(LOADS):
        part = pl.ds(k * span, span)
        loads.append(
            (
                load(pool_hbm.at[0, :, part], pool_ref.at[:, part], 2 + 2 * k),
                load(start_hbm.at[0, part], start_ref.at[part], 3 + 2 * k),
            )
        )
    goal_load = load(goal_hbm.at[0, 0], goal_ref, 1)

    barrier = pltpu.get_barrier_semaphore()

    def x_peer(i):
        return lax.rem(x + i, tall)

    def y_peer(j):
        return lax.rem(y + j, RING)

    def peer_at(place):
        return x_peer(place[0]) * RING + y_peer(place[1])

    for place in OTHERS:
        pl.semaphore_signal(
            barrier,
            inc=1,
            device_id={"rep": peer_at(place), "shard": shard},
            device_id_type=MESH,
        )
    pl.semaphore_signal(
        barrier, inc=1, device_id={"rep": me, "shard": shard ^ 1}, device_id_type=MESH
    )

    def copy(src, dst, send_sem, recv_sem, rep, to_shard=None):
        return pltpu.make_async_remote_copy(
            src_ref=src,
            dst_ref=dst,
            send_sem=send_sem,
            recv_sem=recv_sem,
            device_id={"rep": rep, "shard": shard if to_shard is None else to_shard},
            device_id_type=MESH,
        )

    index_load.wait()
    marks, picks = routing(index_ref[...], pool_count)
    first = square = border = None
    cut = 2 * pool_count // 3
    for k in range(LOADS):
        for part in loads[k]:
            part.wait()
        tokens = pool_ref[:, k * span : (k + 1) * span]
        turned[k * span : (k + 1) * span, :] = tokens.T
        one_first = dot(tokens, start_ref[k * span : (k + 1) * span, :])
        one_square = dot_last(tokens[:cut], tokens[:cut])
        one_border = dot_last(tokens[cut:], tokens)
        first = one_first if first is None else first + one_first
        square = one_square if square is None else square + one_square
        border = one_border if border is None else border + one_border
    upper = jnp.concatenate([square, border[:, :cut].T], axis=1)
    products = jnp.concatenate([upper, border], axis=0)
    goal_load.wait()
    weights = local_steps(first, products, marks, picks, goal_ref, width, gates)

    pl.semaphore_wait(barrier, reps)

    def a2a(peer, h):
        return copy(
            delta.at[pl.ds(pl.multiple_of(peer * seg + starts[h], 16), PARTS[h]), :],
            recv[h].at[me],
            a2a_send.at[0],
            a2a_recv.at[h],
            peer,
        )

    def a2a_all(h):
        count = reps - 1
        return copy(
            recv[h].at[pl.ds(0, count)],
            recv[h].at[pl.ds(0, count)],
            a2a_send.at[0],
            a2a_recv.at[h],
            lax.rem(me + 1, reps),
        )

    order = (4, 1, 7, 3, 5, 2, 6, 0)
    for h in range(len(PARTS)):
        for i in (2, 1, 3, 0):
            if h == 0:
                block = pl.ds(pl.multiple_of(x_peer(i) * RING * seg, RING * seg), RING * seg)
                delta[block, :] = dot(turned[block, :], weights).astype(BF16)
            for j in order:
                if i or j:
                    a2a(peer_at((i, j)), h).start()

    def own(h):
        return pl.ds(pl.multiple_of(me * seg + starts[h], 16), PARTS[h])

    gram = None
    for h, rows in enumerate(PARTS):
        recv[h][me] = delta[own(h), :]
        a2a_all(h).wait_recv()
        for q in range(reps):
            for c in range(cols // 128):
                wide[c, rows * q : rows * q + rows, :] = recv[h][
                    q, :, 128 * c : 128 * c + 128
                ].astype(F32)
        for r in range(rows):
            for c in range(cols // 128):
                part = wide[c, pl.ds(r, reps, stride=rows), :]
                place = r * cols + 128 * c
                operand[:, place : place + 128] = part.astype(BF16)
        sides = operand[:, 0 : rows * cols]
        term = dot_last(sides, sides)
        gram = term if gram is None else gram + term

    gram_pad[...] = jnp.zeros_like(gram_pad)
    gram_pad[:, 0:reps] = gram
    packed = gram_pad[0:8, :]
    for k in range(1, reps // 8):
        packed = packed + pltpu.roll(gram_pad[8 * k : 8 * k + 8, :], reps * k, 1)

    gram_core[core] = packed

    def one(place):
        return copy(
            gram_core.at[core],
            gram_core.at[place],
            one_send.at[0],
            one_recv.at[0],
            me,
            shard ^ 1,
        )

    def two(place):
        return copy(
            gram_all.at[me], gram_all.at[me], two_send.at[0], two_recv.at[0], peer_at(place)
        )

    def two_all():
        every = gram_all.at[pl.ds(0, reps - 1)]
        return copy(every, every, two_send.at[0], two_recv.at[0], peer_at(OTHERS[0]))

    one(core).start()
    one(1 - core).wait_recv()
    gram_all[me] = gram_core[0] + gram_core[1]
    for place in OTHERS:
        two(place).start()
    two_all().wait_recv()
    packed = jnp.sum(gram_all[...], axis=0)
    lane = lax.broadcasted_iota(jnp.int32, packed.shape, 1)
    pieces = [
        jnp.where(lane < reps, packed if k == 0 else pltpu.roll(packed, 128 - reps * k, 1), 0.0)
        for k in range(reps // 8)
    ]
    coef = tree_coefs(jnp.concatenate(pieces, axis=0))
    coefs[...] = jnp.broadcast_to(coef, coefs.shape)

    def finish(h):
        total = jnp.zeros((PARTS[h], cols), F32)
        for q in range(reps):
            total = total + coefs[q : q + 1, :] * recv[h][q].astype(F32)
        combined = total.astype(BF16).astype(F32)
        out_ref[x, y, starts[h] : starts[h] + PARTS[h]] = (
            start_ref[own(h), :].astype(F32) + combined
        ).astype(BF16)

    top = pl.ds(0, PARTS[0])
    low = pl.ds(PARTS[0], PARTS[1])

    def ya(j, arriving):
        p = y_peer(j)
        place = p if arriving else y
        return copy(
            out_ref.at[x, y, top],
            out_ref.at[x, place, top],
            ya_send.at[p],
            ya_recv.at[place],
            x * RING + p,
        )

    def xa(i, j):
        p = x_peer(i)
        chunk = out_ref.at[x, y_peer(j), top]
        return copy(chunk, chunk, xa_send.at[p], xa_recv.at[x], p * RING + y)

    def xa_all(i):
        p = x_peer(i)
        return copy(
            out_ref.at[x, :, top], out_ref.at[p, :, top], xa_send.at[p], xa_recv.at[p], p * RING + y
        )

    def xb(i, arriving):
        p = x_peer(i)
        place = p if arriving else x
        return copy(
            out_ref.at[x, y, low],
            out_ref.at[place, y, low],
            xb_send.at[p],
            xb_recv.at[place],
            p * RING + y,
        )

    def yb(j, arriving):
        p = y_peer(j)
        place = p if arriving else y
        return copy(
            out_ref.at[:, y, low],
            out_ref.at[:, place, low],
            yb_send.at[p],
            yb_recv.at[place],
            x * RING + p,
        )

    near_first = (1, 7, 2, 6, 3, 5, 4)
    far_first = (4, 3, 5, 2, 6, 1, 7)
    across = (2, 1, 3)
    finish(1)
    for i in across:
        xb(i, False).start()
    finish(0)
    for j in near_first:
        ya(j, False).start()
    for i in across:
        xa(i, 0).start()
    for i in range(1, tall):
        xb(i, True).wait_recv()
    for j in far_first:
        yb(j, False).start()
    for j in near_first:
        ya(j, True).wait_recv()
        for i in across:
            xa(i, j).start()
    for j in range(1, RING):
        yb(j, True).wait_recv()
    for i in range(1, tall):
        xa_all(i).wait_recv()

    for h in range(len(PARTS)):
        a2a_all(h).wait_send()
    one(core).wait_send()
    two_all().wait_send()
    for j in range(1, RING):
        ya(j, False).wait_send()
        yb(j, False).wait_send()
    for i in range(1, tall):
        xa_all(i).wait_send()
        xb(i, False).wait_send()


def body(token_pool, row_index, weights, targets):
    reps = lax.axis_size("rep")
    tall = reps // RING
    pool_count, width = token_pool.shape[1:]
    total = row_index.shape[3]
    cols = weights.shape[2]
    seg = width // reps
    dma = pltpu.SemaphoreType.DMA
    out = pl.pallas_call(
        kernel,
        out_shape=jax.ShapeDtypeStruct((tall, RING, seg, cols), BF16),
        in_specs=[pl.BlockSpec(memory_space=pltpu.HBM)] * 4,
        out_specs=pl.BlockSpec(memory_space=pltpu.VMEM),
        scratch_shapes=[
            pltpu.VMEM((pool_count, width), BF16),
            pltpu.VMEM((1, total), jnp.int32),
            pltpu.VMEM((width, cols), BF16),
            pltpu.VMEM((total, cols), BF16),
            pltpu.VMEM((total, cols), BF16),
            pltpu.VMEM((width, pool_count), BF16),
            pltpu.VMEM((width, cols), BF16),
            pltpu.VMEM((reps, PARTS[0], cols), BF16),
            pltpu.VMEM((reps, PARTS[1], cols), BF16),
            pltpu.VMEM((cols // 128, (reps + 1) * PARTS[0], 128), F32),
            pltpu.VMEM((reps, PARTS[0] * cols), BF16),
            pltpu.VMEM((reps, 128), F32),
            pltpu.VMEM((CUT, 8, 128), F32),
            pltpu.VMEM((reps, 8, 128), F32),
            pltpu.VMEM((reps, cols), F32),
            dma((2 + 2 * LOADS,)),
            dma((1,)),
            dma((2,)),
            dma((1,)),
            dma((1,)),
            dma((1,)),
            dma((1,)),
            dma((RING,)),
            dma((RING,)),
            dma((tall,)),
            dma((tall,)),
            dma((tall,)),
            dma((tall,)),
            dma((RING,)),
            dma((RING,)),
        ],
        compiler_params=pltpu.CompilerParams(
            collective_id=0, has_side_effects=True, vmem_limit_bytes=40 * 1024 * 1024
        ),
    )(
        *(
            pltpu.with_memory_space_constraint(array, pltpu.HBM)
            for array in (token_pool, row_index, weights, targets)
        )
    )
    return out.reshape(weights.shape)


def solution(mesh):
    in_specs = (
        P("rep", None, None),
        P("rep", None, None, None),
        P(None, None, "shard"),
        P("rep", None, None, "shard"),
    )
    out_specs = P(None, None, "shard")
    return jax.shard_map(body, mesh=mesh, in_specs=in_specs, out_specs=out_specs, check_vma=False)
```
